32 devices in a mesh: groups: 2 (over y), expert: 16 (over z, x, core).
Axes of the slice: x: 2, y: 2, z: 4, core: 2. Of those that a mesh axis runs over, the one named last changes fastest.
Arguments:
- activations: bfloat16 [2, 512, 2048], P(None, ('groups', 'expert')), parts along dimension 1, may hold values from -6 to 6
- pick_weight: float32 [2, 512, 1], P(None, ('groups', 'expert')), parts along dimension 1, may hold values from 0.2 to 1
- expert_ids: int32 [2, 512, 1], P(None, ('groups', 'expert')), parts along dimension 1, may hold values from 0 to 7, as said below
- replica: int32 [2, 512, 1], P(None, ('groups', 'expert')), parts along dimension 1, may hold values from 0 to 4, as said below
- old_home: int32 [8], replicated, may hold values from 0 to 7, each once
- new_expert: int32 [32], P('groups'), parts along dimension 0, may hold values from 0 to 7, as said below
- gate_panel: bfloat16 [16, 2048, 384], P('expert'), may hold values from -0.125 to 0.125
- up_panel: bfloat16 [16, 2048, 384], P('expert'), may hold values from -0.125 to 0.125
- down_panel: bfloat16 [16, 2048, 384], P('expert'), may hold values from -0.21875 to 0.21875
Outputs:
- layer_output: bfloat16 [2, 512, 2048], P(None, ('groups', 'expert')), parts along dimension 1
- slot_load: int32 [32], P(('groups', 'expert')), parts along dimension 0
The draws below stay inside these ranges and needn't reach their ends.
There are 2 independent parts, one for each index of `groups`. The reference program is written for one: setup_inputs(seed, part) draws one part's arguments, and reference() takes and returns one part's arrays. A program takes and returns all parts, laid end to end along the dimension named above; an argument that names none is the same for every part. Nothing has to cross between parts.
Inputs may be any that keep to these rules, and one draw needn't show every extreme that they name: `new_expert`: every expert is held by 1 or 5 slots. `expert_ids`: the 1 expert that a token names are different. replica[s, t, k] is below the number of slots that new_expert gives to expert_ids[s, t, k]. The picks of the 16 tokens of one device in one batch that land on one slot number at most 2, and in each batch some slot receives exactly 2 from every device.
All inputs are finite; a program needn't handle non-finite values.
Results may differ from the reference program's by a relative error of at most 0.0057.
Values may be sent and summed in bfloat16 or wider, within the bound.
A program may use at most 128 MiB of HBM per device.

```python
import math
from functools import partial
import jax
import jax.numpy as jnp
from jax import lax

D = 2048
FF = 768
HALF = 384
STEPS = 2
TOK_DEV = 16
REPL = 5
SLOTS = 16
EXPERTS = 8
HOT = 2
TOP = 1
CAP = 2
TOKENS = 256


def route_block(key, steady, hot_flags):
    keys = jax.random.split(key, 5)
    shuffled = jax.random.permutation(keys[0], EXPERTS).astype(jnp.int32)
    labels = jnp.arange(EXPERTS, dtype=jnp.int32)
    sort_key = jnp.where(shuffled == steady, -1, labels)
    order = shuffled[jnp.argsort(sort_key, stable=True)]
    hot_length = jax.random.randint(keys[1], (EXPERTS,), REPL * CAP - REPL + 1, REPL * CAP + 1, dtype=jnp.int32)
    cold_length = jax.random.randint(keys[2], (EXPERTS,), 1, CAP + 1, dtype=jnp.int32)
    length = jnp.where(hot_flags, hot_length, cold_length)
    length = jnp.where(labels == steady, CAP, length)
    spans = length[order]
    ends = jnp.cumsum(spans).astype(jnp.int32)
    starts = ends - spans
    places = jnp.arange(TOK_DEV * TOP, dtype=jnp.int32)
    which = jnp.sum((ends[None, :] <= places[:, None]).astype(jnp.int32), axis=1)
    chosen = order[which]
    offset = places - starts[which]
    turn = jax.random.randint(keys[3], (EXPERTS,), 0, REPL, dtype=jnp.int32)
    copy_rank = jnp.where(hot_flags[chosen], (offset + turn[chosen]) % REPL, 0).astype(jnp.int32)
    picked_ids = chosen.reshape(TOP, TOK_DEV).T
    picked_ranks = copy_rank.reshape(TOP, TOK_DEV).T
    token_order = jax.random.permutation(keys[4], TOK_DEV)
    return (picked_ids[token_order], picked_ranks[token_order])


def plan(key):
    keys = jax.random.split(jax.random.fold_in(key, 4242), 3)
    shuffled = jax.random.permutation(keys[0], EXPERTS).astype(jnp.int32)
    listed = jnp.concatenate([shuffled] + [shuffled[:HOT]] * (REPL - 1))
    new_expert = listed[jax.random.permutation(keys[1], SLOTS)].astype(jnp.int32)
    labels = jnp.arange(EXPERTS, dtype=jnp.int32)
    hot_flags = jnp.any(labels[:, None] == shuffled[None, :HOT], axis=1)
    steady = shuffled[HOT]
    block_keys = jax.random.split(keys[2], STEPS * SLOTS)
    picked_ids, picked_ranks = jax.vmap(partial(route_block, steady=steady, hot_flags=hot_flags))(block_keys)
    return (new_expert, picked_ids.reshape(STEPS, TOKENS, TOP).astype(jnp.int32), picked_ranks.reshape(STEPS, TOKENS, TOP).astype(jnp.int32))


def draw_new_expert(key, part):
    return plan(key)[0]


def draw_expert_ids(key, part):
    return plan(key)[1]


def draw_replica(key, part):
    return plan(key)[2]


def steps_of(rng, extent, cuts, smallest, top_value):
    def one(dim, shards_of):
        heights = jax.random.uniform(jax.random.fold_in(jax.random.fold_in(rng, 6), dim), (shards_of,), jnp.float32, smallest / len(cuts), top_value / len(cuts))
        return jnp.repeat(jnp.exp(heights), extent[dim] // shards_of).reshape((-1,) + (1,) * (len(extent) - dim - 1))

    gain = one(*cuts[0])
    for cut in cuts[1:]:
        gain = gain * one(*cut)
    return gain


def normal_values(stream_key, shape, width, bound, cuts=(), kind=jnp.bfloat16):
    array = jax.random.normal(stream_key, shape, jnp.float32) * width
    if len(cuts) > 0:
        array = steps_of(stream_key, shape, cuts, -0.22, 0.18) * array
    return jnp.clip(array, min=-bound, max=bound).astype(kind)


def setup_inputs(seed: int = 0, part: int = 0) -> dict:
    key_list = jax.random.split(jax.random.key(seed), 10)
    part_keys = jax.random.split(jax.random.fold_in(key_list[9], part), 10)
    return {
        "activations": normal_values(part_keys[0], (STEPS, TOKENS, D), 1.0, 6.0, ((1, 16),)),
        "pick_weight": jnp.clip(jnp.exp(math.log(1.0) - 1.609438 * jax.random.uniform(part_keys[1], (STEPS, TOKENS, TOP), jnp.float32) ** steps_of(part_keys[1], (STEPS, TOKENS, TOP), ((1, 16),), -0.2, 0.2)), 0.2, 1.0),
        "expert_ids": draw_expert_ids(jax.random.fold_in(jax.random.fold_in(key_list[9], part), 71), part),
        "replica": draw_replica(jax.random.fold_in(jax.random.fold_in(key_list[9], part), 71), part),
        "old_home": jax.random.permutation(key_list[4], EXPERTS).astype(jnp.int32),
        "new_expert": draw_new_expert(jax.random.fold_in(jax.random.fold_in(key_list[9], part), 71), part),
        "gate_panel": normal_values(key_list[6], (SLOTS, D, HALF), D ** -0.5, 0.125, ((0, 16),)),
        "up_panel": normal_values(key_list[7], (SLOTS, D, HALF), D ** -0.5, 0.125, ((0, 16),)),
        "down_panel": normal_values(key_list[8], (SLOTS, D, HALF), FF ** -0.5, 0.21875, ((0, 16),)),
    }


def expert_weights(panel, old_home, expert):
    home = lax.dynamic_index_in_dim(old_home, expert, 0, keepdims=False)
    both = lax.dynamic_slice_in_dim(panel, (2 * home).astype(jnp.int32), 2, 0)
    return jnp.concatenate((both[0], both[1]), axis=1)


def one_batch(tokens, weights, ids, old_home, gate_panel, up_panel, down_panel):
    block = 128
    count, picks_each = ids.shape
    picks = count * picks_each
    flat_ids = ids.reshape(picks).astype(jnp.int32)
    labels = jnp.arange(EXPERTS, dtype=jnp.int32)
    counts = jnp.sum((flat_ids[:, None] == labels[None, :]).astype(jnp.int32), axis=0).astype(jnp.int32)
    starts = (jnp.cumsum(counts) - counts).astype(jnp.int32)
    blocks_of = ((counts + block - 1) // block).astype(jnp.int32)
    block_end = jnp.cumsum(blocks_of).astype(jnp.int32)
    padded_start = ((block_end - blocks_of) * block).astype(jnp.int32)
    order = jnp.argsort(flat_ids, stable=True).astype(jnp.int32)
    sorted_ids = flat_ids[order]
    rank = (jnp.arange(picks, dtype=jnp.int32) - starts[sorted_ids]).astype(jnp.int32)
    padded_pos = (padded_start[sorted_ids] + rank).astype(jnp.int32)
    total_blocks = (picks + block - 1) // block + EXPERTS
    pad_pick = jnp.full((total_blocks * block,), -1, jnp.int32).at[padded_pos].set(order)
    block_ids = jnp.arange(total_blocks, dtype=jnp.int32)
    reached = (block_ids[:, None] >= block_end[None, :]).astype(jnp.int32)
    block_expert = jnp.minimum(jnp.sum(reached, axis=1), EXPERTS - 1).astype(jnp.int32)

    def run(index):
        expert = block_expert[index]
        members = lax.dynamic_slice_in_dim(pad_pick, (index * block).astype(jnp.int32), block)
        valid = members >= 0
        token_index = jnp.where(valid, members // picks_each, 0).astype(jnp.int32)
        picked = tokens[token_index]
        gate_full = expert_weights(gate_panel, old_home, expert)
        up_full = expert_weights(up_panel, old_home, expert)
        down_full = expert_weights(down_panel, old_home, expert)
        gate = jnp.dot(picked, gate_full, preferred_element_type=jnp.float32)
        up = jnp.dot(picked, up_full, preferred_element_type=jnp.float32)
        hidden = (jax.nn.silu(gate) * up).astype(jnp.bfloat16)
        result = jnp.dot(hidden, down_full.T, preferred_element_type=jnp.float32).astype(jnp.bfloat16)
        return jnp.where(valid[:, None], result, jnp.zeros((), result.dtype))

    results = lax.map(run, block_ids)
    pick_pos = jnp.zeros((picks,), jnp.int32).at[order].set(padded_pos)
    per_pick = results.reshape(-1, tokens.shape[1])[pick_pos].reshape(count, picks_each, -1)
    total = jnp.sum(weights[:, :, None] * per_pick.astype(jnp.float32), axis=1)
    return total.astype(jnp.bfloat16)


def slot_counts(ids, replica, new_expert):
    slots = new_expert.shape[0]
    positions = jnp.arange(slots, dtype=jnp.int32)
    same = new_expert[:, None] == new_expert[None, :]
    ranks = jnp.sum((same & (positions[None, :] < positions[:, None])).astype(jnp.int32), axis=1)
    flat_ids = ids.reshape(-1)
    flat_rep = replica.reshape(-1)
    match = (new_expert[None, :] == flat_ids[:, None]) & (ranks[None, :] == flat_rep[:, None])
    return jnp.sum(match.astype(jnp.int32), axis=0).astype(jnp.int32)


def reference(activations, pick_weight, expert_ids, replica, old_home, new_expert, gate_panel, up_panel, down_panel):
    outputs = []
    slot_load = jnp.zeros((new_expert.shape[0],), jnp.int32)
    for batch in range(STEPS):
        outputs.append(one_batch(activations[batch], pick_weight[batch], expert_ids[batch], old_home, gate_panel, up_panel, down_panel))
        slot_load = slot_load + slot_counts(expert_ids[batch], replica[batch], new_expert)
    return jnp.stack(outputs, axis=0), slot_load.astype(jnp.int32)
```

```python
import functools
import math

import jax
import jax.numpy as jnp
from jax import lax
from jax.experimental import pallas as pl
from jax.experimental.pallas import tpu as pltpu
from jax.sharding import PartitionSpec as P

MESH = pl.DeviceIdType.MESH
LANES = 128
ROWS = 256


def grid_of(devices):
    chips = devices // 2
    lo = max(d for d in range(1, math.isqrt(chips) + 1) if chips % d == 0)
    return chips // lo, lo


def layer_kernel(
    n,
    hi,
    lo,
    act_ref,
    weight_ref,
    ids_ref,
    rep_ref,
    home_ref,
    row_ref,
    col_ref,
    gate_ref,
    up_ref,
    down_ref,
    out_ref,
    load_ref,
    tok,
    wgu,
    wd,
    hid,
    res,
    xbuf,
    comb,
    fin,
    local_sem,
    wd_sem,
    z_send,
    z_recv,
    x_send,
    x_recv,
    s_send,
    s_recv,
    h_send,
    h_recv,
    rx_send,
    rx_recv,
    rz_send,
    rz_recv,
):
    batches, t, width = act_ref.shape
    top = ids_ref.shape[2]
    half = gate_ref.shape[2]
    wide = width // 2
    me = lax.axis_index("expert")
    core = lax.rem(me, 2)
    chip = me // 2
    xi = lax.rem(chip, lo)
    zi = chip // lo

    def index(dz, dx, dc):
        z = lax.rem(zi + dz + hi, hi)
        x = lax.rem(xi + dx + lo, lo)
        c = lax.rem(core + dc, 2)
        return (z * lo + x) * 2 + c

    def rows(device, count=1):
        return pl.ds(pl.multiple_of(device * t, t), count * t)

    def remote(src, dst, send, recv, device):
        copy = pltpu.make_async_remote_copy(
            src_ref=src,
            dst_ref=dst,
            send_sem=send,
            recv_sem=recv,
            device_id={"expert": device},
            device_id_type=MESH,
        )
        copy.start()
        return copy

    def local(src, dst, sem):
        copy = pltpu.make_async_copy(src, dst, sem)
        copy.start()
        return copy

    own_cols = pl.ds(pl.multiple_of(core * half, LANES), half)
    act_copies = [
        local(act_ref.at[g], tok.at[g, rows(me), pl.ds(0, width)], local_sem.at[g])
        for g in range(batches)
    ]
    gate_copy = local(gate_ref.at[0], wgu.at[:, pl.ds(0, half)], local_sem.at[batches])
    up_copy = local(up_ref.at[0], wgu.at[:, pl.ds(half, half)], local_sem.at[batches + 1])
    own_half = pl.ds(pl.multiple_of(core * wide, wide), wide)
    other_half = pl.ds(pl.multiple_of((1 - core) * wide, wide), wide)
    down_copy = local(down_ref.at[0, own_half], wd.at[:, own_cols], local_sem.at[batches + 2])

    peers = [index(dz, 0, dc) for dz in range(hi) for dc in range(2) if dz or dc]
    peers += [index(0, dx, 0) for dx in range(1, lo)]
    barrier = pltpu.get_barrier_semaphore()
    for peer in peers:
        pl.semaphore_signal(barrier, inc=1, device_id={"expert": peer}, device_id_type=MESH)

    row = row_ref[...]
    col = col_ref[...]
    slots = row.shape[1]
    s_lane = lax.broadcasted_iota(jnp.int32, (slots, slots), 1)
    s_row = lax.broadcasted_iota(jnp.int32, (slots, slots), 0)
    earlier = (col == row) & (s_row < s_lane)
    ranks = jnp.sum(earlier.astype(jnp.int32), axis=0, keepdims=True)
    homes = home_ref[...]
    lane_slot = lax.broadcasted_iota(jnp.int32, (t, slots), 1)
    lane_expert = lax.broadcasted_iota(jnp.int32, (t, homes.shape[1]), 1)
    lane = lax.broadcasted_iota(jnp.int32, (t, LANES), 1)
    for g in range(batches):
        marks = jnp.zeros((t, LANES), jnp.float32)
        for k in range(top):
            ids = ids_ref[g, :, k : k + 1]
            rep = rep_ref[g, :, k : k + 1]
            weight = weight_ref[g, :, k : k + 1]
            home = jnp.sum(jnp.where(lane_expert == ids, homes, 0), axis=1, keepdims=True)
            match = (row == ids) & (ranks == rep)
            slot = jnp.sum(jnp.where(match, lane_slot, 0), axis=1, keepdims=True)
            first = weight.astype(jnp.bfloat16).astype(jnp.float32)
            second = (weight - first).astype(jnp.bfloat16).astype(jnp.float32)
            third = weight - first - second
            parts = (home.astype(jnp.float32), slot.astype(jnp.float32), first, second, third)
            for place, part in enumerate(parts):
                marks = jnp.where(lane == place * top + k, part, marks)
        tok[g, rows(me), pl.ds(width, LANES)] = marks.astype(jnp.bfloat16)

    pl.semaphore_wait(barrier, len(peers))

    pending = []
    pending.append(
        remote(down_ref.at[0, other_half], wd.at[:, own_cols], wd_sem.at[0], wd_sem.at[1], index(0, 0, 1))
    )

    def forward(g, dz, dx):
        block = tok.at[g, rows(index(-dz, -dx, 0))]
        pending.append(
            remote(block, block, s_send.at[g, dz, dx], s_recv.at[g, dz, dx], index(0, 0, 1))
        )

    def across(g, dz):
        block = tok.at[g, rows(index(-dz, 0, 0))]
        for dx in range(1, lo):
            pending.append(
                remote(
                    block, block, x_send.at[g, dz, dx], x_recv.at[g, dz, dx], index(0, dx, 0)
                )
            )
        forward(g, dz, 0)

    def arrived(ref, send, recv):
        pltpu.make_async_remote_copy(
            src_ref=ref,
            dst_ref=ref,
            send_sem=send,
            recv_sem=recv,
            device_id={"expert": index(0, 0, 1)},
            device_id_type=MESH,
        ).wait_recv()

    def send_z(g):
        act_copies[g].wait()
        block = tok.at[g, rows(me)]
        for dz in range(1, hi):
            pending.append(
                remote(block, block, z_send.at[g, dz], z_recv.at[g, dz], index(dz, 0, 0))
            )
        across(g, 0)

    def relay_z(g):
        for dz in range(1, hi):
            arrived(tok.at[g, rows(index(-dz, 0, 0))], z_send.at[g, dz], z_recv.at[g, dz])
            across(g, dz)

    def relay_x(g):
        for dz in range(hi):
            for dx in range(1, lo):
                arrived(
                    tok.at[g, rows(index(-dz, -dx, 0))],
                    x_send.at[g, dz, dx],
                    x_recv.at[g, dz, dx],
                )
                forward(g, dz, dx)

    def await_all(g):
        for dz in range(hi):
            for dx in range(lo):
                arrived(
                    tok.at[g, rows(index(-dz, -dx, 1))],
                    s_send.at[g, dz, dx],
                    s_recv.at[g, dz, dx],
                )

    total = n * t
    step = min(ROWS, total)

    def chunks(body):
        if total == step:
            body(pl.ds(0, step))
        else:

            @pl.loop(0, total // step)
            def _(i):
                body(pl.ds(pl.multiple_of(i * step, step), step))

    def hidden(g):
        def body(part):
            both = jnp.dot(
                tok[g, part, pl.ds(0, width)], wgu[...], preferred_element_type=jnp.float32
            )
            gate, up = both[:, :half], both[:, half:]
            value = gate / (1.0 + jnp.exp(-gate)) * up
            hid[g, part, own_cols] = value.astype(jnp.bfloat16)

        chunks(body)
        mine = hid.at[g, :, own_cols]
        pending.append(remote(mine, mine, h_send.at[g], h_recv.at[g], index(0, 0, 1)))

    def result(g):
        other_cols = pl.ds(pl.multiple_of((1 - core) * half, LANES), half)
        arrived(hid.at[g, :, other_cols], h_send.at[g], h_recv.at[g])

        def body(part):
            value = lax.dot_general(
                hid[g, part, :],
                wd[...],
                (((1,), (1,)), ((), ())),
                preferred_element_type=jnp.float32,
            )
            value = value.astype(jnp.bfloat16).astype(jnp.float32)
            marks = tok[g, part, pl.ds(width, LANES)].astype(jnp.float32)
            scale = jnp.zeros((step, 1), jnp.float32)
            for k in range(top):
                home, _, first, second, third = (
                    marks[:, p * top + k : p * top + k + 1] for p in range(5)
                )
                weight = first + (second + third)
                scale += jnp.where(home == chip.astype(jnp.float32), weight, 0.0)
            res[g, part, :] = (value * scale).astype(jnp.bfloat16)

        chunks(body)
        for dz in list(range(1, hi)) + [0]:
            for dx in range(1, lo):
                pending.append(
                    remote(
                        res.at[g, rows(index(dz, dx, 0) - core, 2)],
                        xbuf.at[g, dx, dz],
                        rx_send.at[g, dz, dx],
                        rx_recv.at[g, dz, dx],
                        index(0, dx, 0),
                    )
                )

    def collect(g):
        for dz in list(range(1, hi)) + [0]:
            value = res[g, rows(index(dz, 0, 0) - core, 2), :].astype(jnp.float32)
            for dx in range(1, lo):
                arrived(xbuf.at[g, dx, dz], rx_send.at[g, dz, dx], rx_recv.at[g, dz, dx])
                value += xbuf[g, dx, dz].astype(jnp.float32)
            comb[g, dz] = value.astype(jnp.bfloat16)
            for dc in range(2):
                block = comb.at[g, dz, pl.ds(pl.multiple_of(lax.rem(core + dc, 2) * t, t), t)]
                if dz or dc:
                    pending.append(
                        remote(
                            block,
                            fin.at[g, dz, core],
                            rz_send.at[g, dz, dc],
                            rz_recv.at[g, dz, dc],
                            index(dz, 0, dc),
                        )
                    )
                else:
                    fin[g, dz, core] = block[...]

    def finish(g):
        for dz in range(hi):
            for dc in range(2):
                if dz or dc:
                    arrived(
                        fin.at[g, dz, lax.rem(core + dc, 2)],
                        rz_send.at[g, dz, dc],
                        rz_recv.at[g, dz, dc],
                    )
        for c in range(2):
            value = fin[g, 0, c].astype(jnp.float32)
            for dz in range(1, hi):
                value += fin[g, dz, c].astype(jnp.float32)
            out_ref[g, :, pl.ds(c * wide, wide)] = value.astype(jnp.bfloat16)

    send_z(0)
    relay_z(0)
    for g in range(1, batches):
        send_z(g)
    relay_x(0)
    gate_copy.wait()
    up_copy.wait()
    await_all(0)
    hidden(0)
    down_copy.wait()
    arrived(wd.at[:, own_cols], wd_sem.at[0], wd_sem.at[1])
    for g in range(batches):
        if g + 1 < batches:
            relay_z(g + 1)
        result(g)
        if g + 1 < batches:
            relay_x(g + 1)
            await_all(g + 1)
            hidden(g + 1)
        collect(g)

    count = jnp.zeros((1, 1), jnp.float32)
    for g in range(batches):
        marks = tok[g, :, pl.ds(width, LANES)].astype(jnp.float32)
        place = lax.broadcasted_iota(jnp.int32, marks.shape, 1)
        mine = (place >= top) & (place < 2 * top) & (marks == me.astype(jnp.float32))
        per_lane = jnp.sum(jnp.where(mine, 1.0, 0.0), axis=0, keepdims=True)
        count += jnp.sum(per_lane, axis=1, keepdims=True)
    load_ref[...] = count.astype(jnp.int32)

    for g in range(batches):
        finish(g)
    for copy in pending:
        copy.wait_send()


def per_device(
    activations,
    pick_weight,
    expert_ids,
    replica,
    old_home,
    new_expert,
    gate_panel,
    up_panel,
    down_panel,
):
    n = lax.axis_size("expert")
    hi, lo = grid_of(n)
    batches, t, width = activations.shape
    half = gate_panel.shape[2]
    wide = width // 2
    total = n * t
    dma = pltpu.SemaphoreType.DMA
    vmem = pl.BlockSpec(memory_space=pltpu.VMEM)
    hbm = pl.BlockSpec(memory_space=pl.ANY)
    bf16 = jnp.bfloat16
    out, load = pl.pallas_call(
        functools.partial(layer_kernel, n, hi, lo),
        out_shape=(
            jax.ShapeDtypeStruct(activations.shape, bf16),
            jax.ShapeDtypeStruct((1, 1), jnp.int32),
        ),
        in_specs=[hbm, vmem, vmem, vmem, vmem, vmem, vmem, hbm, hbm, hbm],
        out_specs=(vmem, vmem),
        scratch_shapes=[
            pltpu.VMEM((batches, total, width + LANES), bf16),
            pltpu.VMEM((width, 2 * half), bf16),
            pltpu.VMEM((wide, 2 * half), bf16),
            pltpu.VMEM((batches, total, 2 * half), bf16),
            pltpu.VMEM((batches, total, wide), bf16),
            pltpu.VMEM((batches, lo, hi, 2 * t, wide), bf16),
            pltpu.VMEM((batches, hi, 2 * t, wide), bf16),
            pltpu.VMEM((batches, hi, 2, t, wide), bf16),
            dma((batches + 3,)),
            dma((2,)),
            dma((batches, hi)),
            dma((batches, hi)),
            dma((batches, hi, lo)),
            dma((batches, hi, lo)),
            dma((batches, hi, lo)),
            dma((batches, hi, lo)),
            dma((batches,)),
            dma((batches,)),
            dma((batches, hi, lo)),
            dma((batches, hi, lo)),
            dma((batches, hi, 2)),
            dma((batches, hi, 2)),
        ],
        compiler_params=pltpu.CompilerParams(
            collective_id=0, has_side_effects=True, vmem_limit_bytes=60 * 1024 * 1024
        ),
        cost_estimate=pl.CostEstimate(
            flops=6 * batches * total * width * half,
            bytes_accessed=6 * width * half,
            transcendentals=batches * total * half,
        ),
        name="expert_layer",
    )(
        activations,
        pick_weight,
        expert_ids,
        replica,
        old_home.reshape(1, -1),
        new_expert.reshape(1, -1),
        new_expert.reshape(-1, 1),
        gate_panel,
        up_panel,
        down_panel,
    )
    return out, load.reshape(1)


def solution(mesh):
    return jax.shard_map(
        per_device,
        mesh=mesh,
        in_specs=(
            P(None, ("groups", "expert"), None),
            P(None, ("groups", "expert"), None),
            P(None, ("groups", "expert"), None),
            P(None, ("groups", "expert"), None),
            P(),
            P("groups"),
            P("expert", None, None),
            P("expert", None, None),
            P("expert", None, None),
        ),
        out_specs=(P(None, ("groups", "expert"), None), P(("groups", "expert"))),
        check_vma=False,
    )
```

```python
import functools
import math

import jax
import jax.numpy as jnp
from jax import lax
from jax.experimental import pallas as pl
from jax.experimental.pallas import tpu as pltpu
from jax.sharding import PartitionSpec as P

MESH = pl.DeviceIdType.MESH
LANES = 128
ROWS = 256


def grid_of(devices):
    chips = devices // 2
    lo = max(d for d in range(1, math.isqrt(chips) + 1) if chips % d == 0)
    return chips // lo, lo


def layer_kernel(
    hi,
    lo,
    act_ref,
    weight_ref,
    ids_ref,
    rep_ref,
    home_ref,
    row_ref,
    gate_ref,
    up_ref,
    down_ref,
    out_ref,
    load_ref,
    tok,
    wgu,
    wd,
    res,
    xbuf,
    comb,
    fin,
    tally,
    local_sem,
    panel_send,
    panel_recv,
    z_send,
    z_recv,
    x_send,
    x_recv,
    rx_send,
    rx_recv,
    rz_send,
    rz_recv,
    tally_sem,
):
    batches, t, width = act_ref.shape
    top = ids_ref.shape[1]
    half = gate_ref.shape[2]
    full = 2 * half
    me = lax.axis_index("expert")
    core = lax.rem(me, 2)
    chip = me // 2
    xi = lax.rem(chip, lo)
    zi = chip // lo
    sibling = chip * 2 + (1 - core)

    def chip_at(dz, dx):
        z = lax.rem(zi + dz + hi, hi)
        x = lax.rem(xi + dx + lo, lo)
        return z * lo + x

    def device_at(dz, dx):
        return chip_at(dz, dx) * 2 + core

    def rows(place):
        return pl.ds(pl.multiple_of(place * t, t), t)

    def remote(src, dst, send, recv, device):
        copy = pltpu.make_async_remote_copy(
            src_ref=src,
            dst_ref=dst,
            send_sem=send,
            recv_sem=recv,
            device_id={"expert": device},
            device_id_type=MESH,
        )
        copy.start()
        return copy

    def arrived(ref, send, recv):
        pltpu.make_async_remote_copy(
            src_ref=ref,
            dst_ref=ref,
            send_sem=send,
            recv_sem=recv,
            device_id={"expert": sibling},
            device_id_type=MESH,
        ).wait_recv()

    def local(src, dst, sem):
        copy = pltpu.make_async_copy(src, dst, sem)
        copy.start()
        return copy

    peers = [device_at(dz, 0) for dz in range(1, hi)]
    peers += [device_at(0, dx) for dx in range(1, lo)] + [sibling]
    barrier = pltpu.get_barrier_semaphore()
    for peer in peers:
        pl.semaphore_signal(barrier, inc=1, device_id={"expert": peer}, device_id_type=MESH)

    gate_cols = pl.ds(pl.multiple_of(core * half, LANES), half)
    up_cols = pl.ds(pl.multiple_of(full + core * half, LANES), half)
    panels = (
        (gate_ref.at[0], wgu.at[:, gate_cols]),
        (up_ref.at[0], wgu.at[:, up_cols]),
        (down_ref.at[0], wd.at[:, gate_cols]),
    )
    act_copies = [
        local(act_ref.at[g], tok.at[g, rows(chip), pl.ds(0, width)], local_sem.at[g])
        for g in range(batches)
    ]
    panel_copies = [
        local(src, dst, local_sem.at[batches + p]) for p, (src, dst) in enumerate(panels)
    ]

    def upright(line):
        count = line.shape[1]
        shape = (count, count)
        same = lax.broadcasted_iota(jnp.int32, shape, 0) == lax.broadcasted_iota(
            jnp.int32, shape, 1
        )
        return jnp.sum(jnp.where(same, line, jnp.zeros_like(line)), axis=1, keepdims=True)

    row = row_ref[...]
    slots = row.shape[1]
    s_lane = lax.broadcasted_iota(jnp.int32, (slots, slots), 1)
    s_row = lax.broadcasted_iota(jnp.int32, (slots, slots), 0)
    earlier = (upright(row) == row) & (s_row < s_lane)
    ranks = jnp.sum(earlier.astype(jnp.int32), axis=0, keepdims=True)
    homes = home_ref[...]
    lane_slot = lax.broadcasted_iota(jnp.int32, (t, slots), 1)
    lane_expert = lax.broadcasted_iota(jnp.int32, (t, homes.shape[1]), 1)
    lane = lax.broadcasted_iota(jnp.int32, (t, LANES), 1)
    for g in range(batches):
        marks = jnp.zeros((t, LANES), jnp.float32)
        for k in range(top):
            ids = upright(ids_ref[g, k : k + 1, :])
            rep = upright(rep_ref[g, k : k + 1, :])
            weight = upright(weight_ref[g, k : k + 1, :])
            home = jnp.sum(jnp.where(lane_expert == ids, homes, 0), axis=1, keepdims=True)
            match = (row == ids) & (ranks == rep)
            slot = jnp.sum(jnp.where(match, lane_slot, 0), axis=1, keepdims=True)
            first = weight.astype(jnp.bfloat16).astype(jnp.float32)
            second = (weight - first).astype(jnp.bfloat16).astype(jnp.float32)
            third = weight - first - second
            parts = (home.astype(jnp.float32), slot.astype(jnp.float32), first, second, third)
            for place, part in enumerate(parts):
                marks = jnp.where(lane == place * top + k, part, marks)
        tok[g, rows(chip), pl.ds(width, LANES)] = marks.astype(jnp.bfloat16)

    pl.semaphore_wait(barrier, len(peers))

    pending = []

    def across(g, dz):
        block = tok.at[g, rows(chip_at(-dz, 0))]
        for dx in range(1, lo):
            pending.append(
                remote(
                    block, block, x_send.at[g, dz, dx], x_recv.at[g, dz, dx], device_at(0, dx)
                )
            )

    def send_z(g):
        act_copies[g].wait()
        block = tok.at[g, rows(chip)]
        for dz in range(1, hi):
            pending.append(
                remote(block, block, z_send.at[g, dz], z_recv.at[g, dz], device_at(dz, 0))
            )
        across(g, 0)

    def relay_z(g):
        for dz in range(1, hi):
            arrived(tok.at[g, rows(chip_at(-dz, 0))], z_send.at[g, dz], z_recv.at[g, dz])
            across(g, dz)

    def await_x(g):
        for dz in range(hi):
            for dx in range(1, lo):
                arrived(
                    tok.at[g, rows(chip_at(-dz, -dx))],
                    x_send.at[g, dz, dx],
                    x_recv.at[g, dz, dx],
                )

    total = hi * lo * t
    step = min(ROWS, total)

    def expert(g):
        def body(part):
            both = jnp.dot(
                tok[g, part, pl.ds(0, width)], wgu[...], preferred_element_type=jnp.float32
            )
            gate, up = both[:, :full], both[:, full:]
            hidden = (gate / (1.0 + jnp.exp(-gate)) * up).astype(jnp.bfloat16)
            value = lax.dot_general(
                hidden, wd[...], (((1,), (1,)), ((), ())), preferred_element_type=jnp.float32
            )
            value = value.astype(jnp.bfloat16).astype(jnp.float32)
            marks = tok[g, part, pl.ds(width, LANES)].astype(jnp.float32)
            scale = jnp.zeros((step, 1), jnp.float32)
            for k in range(top):
                home, _, first, second, third = (
                    marks[:, p * top + k : p * top + k + 1] for p in range(5)
                )
                weight = first + (second + third)
                scale += jnp.where(home == chip.astype(jnp.float32), weight, 0.0)
            res[g, part, :] = (value * scale).astype(jnp.bfloat16)

        if total == step:
            body(pl.ds(0, step))
        else:

            @pl.loop(0, total // step)
            def _(i):
                body(pl.ds(pl.multiple_of(i * step, step), step))

        for dz in back_order:
            for dx in range(1, lo):
                pending.append(
                    remote(
                        res.at[g, rows(chip_at(dz, dx))],
                        xbuf.at[g, dx, dz],
                        rx_send.at[g, dz, dx],
                        rx_recv.at[g, dz, dx],
                        device_at(0, dx),
                    )
                )

    back_order = list(range(1, hi)) + [0]

    def collect(g):
        for dz in back_order:
            value = res[g, rows(chip_at(dz, 0)), :].astype(jnp.float32)
            for dx in range(1, lo):
                arrived(xbuf.at[g, dx, dz], rx_send.at[g, dz, dx], rx_recv.at[g, dz, dx])
                value += xbuf[g, dx, dz].astype(jnp.float32)
            if dz:
                comb[g, dz] = value.astype(jnp.bfloat16)
                pending.append(
                    remote(
                        comb.at[g, dz],
                        fin.at[g, dz],
                        rz_send.at[g, dz],
                        rz_recv.at[g, dz],
                        device_at(dz, 0),
                    )
                )
            else:
                fin[g, 0] = value.astype(jnp.bfloat16)

    def finish(g):
        value = fin[g, 0].astype(jnp.float32)
        for dz in range(1, hi):
            arrived(fin.at[g, dz], rz_send.at[g, dz], rz_recv.at[g, dz])
            value += fin[g, dz].astype(jnp.float32)
        out_ref[g] = value.astype(jnp.bfloat16)

    def picks_of(slot):
        count = jnp.zeros((1, 1), jnp.float32)
        for g in range(batches):
            marks = tok[g, :, pl.ds(width, LANES)].astype(jnp.float32)
            place = lax.broadcasted_iota(jnp.int32, marks.shape, 1)
            mine = (place >= top) & (place < 2 * top) & (marks == slot.astype(jnp.float32))
            per_lane = jnp.sum(jnp.where(mine, 1.0, 0.0), axis=0, keepdims=True)
            count += jnp.sum(per_lane, axis=1, keepdims=True)
        return count

    send_z(0)
    pushed = [
        remote(src, dst, panel_send.at[p], panel_recv.at[p], sibling)
        for p, (src, dst) in enumerate(panels)
    ]
    pending.extend(pushed)
    relay_z(0)
    for g in range(1, batches):
        send_z(g)
    await_x(0)
    for p, (copy, (_, dst)) in enumerate(zip(panel_copies, panels)):
        copy.wait()
        other_cols = (
            wgu.at[:, pl.ds(pl.multiple_of((1 - core) * half, LANES), half)],
            wgu.at[:, pl.ds(pl.multiple_of(full + (1 - core) * half, LANES), half)],
            wd.at[:, pl.ds(pl.multiple_of((1 - core) * half, LANES), half)],
        )[p]
        arrived(other_cols, panel_send.at[p], panel_recv.at[p])
    for g in range(batches):
        if g + 1 < batches:
            relay_z(g + 1)
        expert(g)
        if g + 1 < batches:
            await_x(g + 1)
        collect(g)

    tally[0] = jnp.broadcast_to(picks_of(sibling), tally.shape[1:])
    swap = remote(tally.at[0], tally.at[1], tally_sem.at[0], tally_sem.at[1], sibling)
    pending.append(swap)
    count = picks_of(me)
    for g in range(batches):
        finish(g)
    arrived(tally.at[1], tally_sem.at[0], tally_sem.at[1])
    load_ref[...] = (count + tally[1, :1, :1]).astype(jnp.int32)
    for copy in pending:
        copy.wait_send()


def per_device(
    activations,
    pick_weight,
    expert_ids,
    replica,
    old_home,
    new_expert,
    gate_panel,
    up_panel,
    down_panel,
):
    n = lax.axis_size("expert")
    hi, lo = grid_of(n)
    batches, t, width = activations.shape
    half = gate_panel.shape[2]
    total = hi * lo * t
    dma = pltpu.SemaphoreType.DMA
    vmem = pl.BlockSpec(memory_space=pltpu.VMEM)
    hbm = pl.BlockSpec(memory_space=pl.ANY)
    bf16 = jnp.bfloat16
    out, load = pl.pallas_call(
        functools.partial(layer_kernel, hi, lo),
        out_shape=(
            jax.ShapeDtypeStruct(activations.shape, bf16),
            jax.ShapeDtypeStruct((1, 1), jnp.int32),
        ),
        in_specs=[hbm, vmem, vmem, vmem, vmem, vmem, hbm, hbm, hbm],
        out_specs=(vmem, vmem),
        scratch_shapes=[
            pltpu.VMEM((batches, total, width + LANES), bf16),
            pltpu.VMEM((width, 4 * half), bf16),
            pltpu.VMEM((width, 2 * half), bf16),
            pltpu.VMEM((batches, total, width), bf16),
            pltpu.VMEM((batches, lo, hi, t, width), bf16),
            pltpu.VMEM((batches, hi, t, width), bf16),
            pltpu.VMEM((batches, hi, t, width), bf16),
            pltpu.VMEM((2, 8, LANES), jnp.float32),
            dma((batches + 3,)),
            dma((3,)),
            dma((3,)),
            dma((batches, hi)),
            dma((batches, hi)),
            dma((batches, hi, lo)),
            dma((batches, hi, lo)),
            dma((batches, hi, lo)),
            dma((batches, hi, lo)),
            dma((batches, hi)),
            dma((batches, hi)),
            dma((2,)),
        ],
        compiler_params=pltpu.CompilerParams(
            collective_id=0, has_side_effects=True, vmem_limit_bytes=60 * 1024 * 1024
        ),
        cost_estimate=pl.CostEstimate(
            flops=12 * batches * total * width * half,
            bytes_accessed=12 * width * half,
            transcendentals=2 * batches * total * half,
        ),
        name="expert_layer",
    )(
        activations,
        pick_weight.transpose(0, 2, 1),
        expert_ids.transpose(0, 2, 1),
        replica.transpose(0, 2, 1),
        old_home.reshape(1, -1),
        new_expert.reshape(1, -1),
        gate_panel,
        up_panel,
        down_panel,
    )
    return out, load.reshape(1)


def solution(mesh):
    return jax.shard_map(
        per_device,
        mesh=mesh,
        in_specs=(
            P(None, ("groups", "expert"), None),
            P(None, ("groups", "expert"), None),
            P(None, ("groups", "expert"), None),
            P(None, ("groups", "expert"), None),
            P(),
            P("groups"),
            P("expert", None, None),
            P("expert", None, None),
            P("expert", None, None),
        ),
        out_specs=(P(None, ("groups", "expert"), None), P(("groups", "expert"))),
        check_vma=False,
    )
```

```python
import functools
import math

import jax
import jax.numpy as jnp
from jax import lax
from jax.experimental import pallas as pl
from jax.experimental.pallas import tpu as pltpu
from jax.sharding import PartitionSpec as P

MESH = pl.DeviceIdType.MESH
LANES = 128
ROWS = 256


def grid_of(devices):
    chips = devices // 2
    lo = max(d for d in range(1, math.isqrt(chips) + 1) if chips % d == 0)
    return chips // lo, lo


def layer_kernel(
    hi,
    lo,
    act_ref,
    weight_ref,
    ids_ref,
    rep_ref,
    home_ref,
    row_ref,
    gate_ref,
    up_ref,
    down_ref,
    out_ref,
    load_ref,
    tok,
    wgu,
    wd,
    hid,
    res,
    xbuf,
    comb,
    fin,
    tally,
    local_sem,
    panel_send,
    panel_recv,
    z_send,
    z_recv,
    x_send,
    x_recv,
    rx_send,
    rx_recv,
    rz_send,
    rz_recv,
    tally_sem,
):
    batches, t, width = act_ref.shape
    top = ids_ref.shape[1]
    half = gate_ref.shape[2]
    full = 2 * half
    me = lax.axis_index("expert")
    core = lax.rem(me, 2)
    chip = me // 2
    xi = lax.rem(chip, lo)
    zi = chip // lo
    sibling = chip * 2 + (1 - core)

    def chip_at(dz, dx):
        z = lax.rem(zi + dz + hi, hi)
        x = lax.rem(xi + dx + lo, lo)
        return z * lo + x

    def device_at(dz, dx):
        return chip_at(dz, dx) * 2 + core

    def rows(place):
        return pl.ds(pl.multiple_of(place * t, t), t)

    def remote(src, dst, send, recv, device):
        copy = pltpu.make_async_remote_copy(
            src_ref=src,
            dst_ref=dst,
            send_sem=send,
            recv_sem=recv,
            device_id={"expert": device},
            device_id_type=MESH,
        )
        copy.start()
        return copy

    def arrived(ref, send, recv):
        pltpu.make_async_remote_copy(
            src_ref=ref,
            dst_ref=ref,
            send_sem=send,
            recv_sem=recv,
            device_id={"expert": sibling},
            device_id_type=MESH,
        ).wait_recv()

    def local(src, dst, sem):
        copy = pltpu.make_async_copy(src, dst, sem)
        copy.start()
        return copy

    peers = [device_at(dz, 0) for dz in range(1, hi)]
    peers += [device_at(0, dx) for dx in range(1, lo)] + [sibling]
    barrier = pltpu.get_barrier_semaphore()
    for peer in peers:
        pl.semaphore_signal(barrier, inc=1, device_id={"expert": peer}, device_id_type=MESH)

    gate_cols = pl.ds(pl.multiple_of(core * half, LANES), half)
    up_cols = pl.ds(pl.multiple_of(full + core * half, LANES), half)
    panels = (
        (gate_ref.at[0], wgu.at[:, gate_cols]),
        (up_ref.at[0], wgu.at[:, up_cols]),
        (down_ref.at[0], wd.at[:, gate_cols]),
    )
    act_copies = [
        local(act_ref.at[g], tok.at[g, rows(chip), pl.ds(0, width)], local_sem.at[g])
        for g in range(batches)
    ]
    panel_copies = [
        local(src, dst, local_sem.at[batches + p]) for p, (src, dst) in enumerate(panels)
    ]

    def upright(line):
        count = line.shape[1]
        shape = (count, count)
        same = lax.broadcasted_iota(jnp.int32, shape, 0) == lax.broadcasted_iota(
            jnp.int32, shape, 1
        )
        return jnp.sum(jnp.where(same, line, jnp.zeros_like(line)), axis=1, keepdims=True)

    row = row_ref[...]
    slots = row.shape[1]
    s_lane = lax.broadcasted_iota(jnp.int32, (slots, slots), 1)
    s_row = lax.broadcasted_iota(jnp.int32, (slots, slots), 0)
    earlier = (upright(row) == row) & (s_row < s_lane)
    ranks = jnp.sum(earlier.astype(jnp.int32), axis=0, keepdims=True)
    homes = home_ref[...]
    lane_slot = lax.broadcasted_iota(jnp.int32, (t, slots), 1)
    lane_expert = lax.broadcasted_iota(jnp.int32, (t, homes.shape[1]), 1)
    lane = lax.broadcasted_iota(jnp.int32, (t, LANES), 1)
    for g in range(batches):
        marks = jnp.zeros((t, LANES), jnp.float32)
        for k in range(top):
            ids = upright(ids_ref[g, k : k + 1, :])
            rep = upright(rep_ref[g, k : k + 1, :])
            weight = upright(weight_ref[g, k : k + 1, :])
            home = jnp.sum(jnp.where(lane_expert == ids, homes, 0), axis=1, keepdims=True)
            match = (row == ids) & (ranks == rep)
            slot = jnp.sum(jnp.where(match, lane_slot, 0), axis=1, keepdims=True)
            first = weight.astype(jnp.bfloat16).astype(jnp.float32)
            second = (weight - first).astype(jnp.bfloat16).astype(jnp.float32)
            third = weight - first - second
            parts = (home.astype(jnp.float32), slot.astype(jnp.float32), first, second, third)
            for place, part in enumerate(parts):
                marks = jnp.where(lane == place * top + k, part, marks)
        tok[g, rows(chip), pl.ds(width, LANES)] = marks.astype(jnp.bfloat16)

    pl.semaphore_wait(barrier, len(peers))

    pending = []

    def across(g, dz):
        block = tok.at[g, rows(chip_at(-dz, 0))]
        for dx in range(1, lo):
            pending.append(
                remote(
                    block, block, x_send.at[g, dz, dx], x_recv.at[g, dz, dx], device_at(0, dx)
                )
            )

    def send_z(g):
        act_copies[g].wait()
        block = tok.at[g, rows(chip)]
        for dz in range(1, hi):
            pending.append(
                remote(block, block, z_send.at[g, dz], z_recv.at[g, dz], device_at(dz, 0))
            )
        across(g, 0)

    def relay_z(g):
        for dz in range(1, hi):
            arrived(tok.at[g, rows(chip_at(-dz, 0))], z_send.at[g, dz], z_recv.at[g, dz])
            across(g, dz)

    def await_x(g):
        for dz in range(hi):
            for dx in range(1, lo):
                arrived(
                    tok.at[g, rows(chip_at(-dz, -dx))],
                    x_send.at[g, dz, dx],
                    x_recv.at[g, dz, dx],
                )

    total = hi * lo * t
    step = min(ROWS, total)

    def chunks(body):
        if total == step:
            body(pl.ds(0, step))
        else:

            @pl.loop(0, total // step)
            def _(i):
                body(pl.ds(pl.multiple_of(i * step, step), step))

    def hidden(g):
        def body(part):
            both = jnp.dot(
                tok[g, part, pl.ds(0, width)], wgu[...], preferred_element_type=jnp.float32
            )
            gate, up = both[:, :full], both[:, full:]
            hid[g, part, :] = (gate / (1.0 + jnp.exp(-gate)) * up).astype(jnp.bfloat16)

        chunks(body)

    def result(g):
        def body(part):
            value = lax.dot_general(
                hid[g, part, :],
                wd[...],
                (((1,), (1,)), ((), ())),
                preferred_element_type=jnp.float32,
            )
            value = value.astype(jnp.bfloat16).astype(jnp.float32)
            marks = tok[g, part, pl.ds(width, LANES)].astype(jnp.float32)
            scale = jnp.zeros((step, 1), jnp.float32)
            for k in range(top):
                home, _, first, second, third = (
                    marks[:, p * top + k : p * top + k + 1] for p in range(5)
                )
                weight = first + (second + third)
                scale += jnp.where(home == chip.astype(jnp.float32), weight, 0.0)
            res[g, part, :] = (value * scale).astype(jnp.bfloat16)

        chunks(body)
        for dz in back_order:
            for dx in range(1, lo):
                pending.append(
                    remote(
                        res.at[g, rows(chip_at(dz, dx))],
                        xbuf.at[g, dx, dz],
                        rx_send.at[g, dz, dx],
                        rx_recv.at[g, dz, dx],
                        device_at(0, dx),
                    )
                )

    back_order = list(range(1, hi)) + [0]

    def collect(g):
        for dz in back_order:
            value = res[g, rows(chip_at(dz, 0)), :].astype(jnp.float32)
            for dx in range(1, lo):
                arrived(xbuf.at[g, dx, dz], rx_send.at[g, dz, dx], rx_recv.at[g, dz, dx])
                value += xbuf[g, dx, dz].astype(jnp.float32)
            if dz:
                comb[g, dz] = value.astype(jnp.bfloat16)
                pending.append(
                    remote(
                        comb.at[g, dz],
                        fin.at[g, dz],
                        rz_send.at[g, dz],
                        rz_recv.at[g, dz],
                        device_at(dz, 0),
                    )
                )
            else:
                fin[g, 0] = value.astype(jnp.bfloat16)

    def finish(g):
        value = fin[g, 0].astype(jnp.float32)
        for dz in range(1, hi):
            arrived(fin.at[g, dz], rz_send.at[g, dz], rz_recv.at[g, dz])
            value += fin[g, dz].astype(jnp.float32)
        out_ref[g] = value.astype(jnp.bfloat16)

    def await_panel(p):
        panel_copies[p].wait()
        first = pl.multiple_of((1 - core) * half, LANES)
        if p == 0:
            ref = wgu.at[:, pl.ds(first, half)]
        elif p == 1:
            ref = wgu.at[:, pl.ds(pl.multiple_of(full + first, LANES), half)]
        else:
            ref = wd.at[:, pl.ds(first, half)]
        arrived(ref, panel_send.at[p], panel_recv.at[p])

    def picks_of(slot):
        count = jnp.zeros((1, 1), jnp.float32)
        for g in range(batches):
            marks = tok[g, :, pl.ds(width, LANES)].astype(jnp.float32)
            place = lax.broadcasted_iota(jnp.int32, marks.shape, 1)
            mine = (place >= top) & (place < 2 * top) & (marks == slot.astype(jnp.float32))
            per_lane = jnp.sum(jnp.where(mine, 1.0, 0.0), axis=0, keepdims=True)
            count += jnp.sum(per_lane, axis=1, keepdims=True)
        return count

    send_z(0)
    pushed = [
        remote(src, dst, panel_send.at[p], panel_recv.at[p], sibling)
        for p, (src, dst) in enumerate(panels)
    ]
    pending.extend(pushed)
    relay_z(0)
    for g in range(1, batches):
        send_z(g)
    await_x(0)
    for g in range(batches):
        if g == 0:
            await_panel(0)
            await_panel(1)
        hidden(g)
        if g == 0:
            await_panel(2)
        result(g)
        if g + 1 < batches:
            relay_z(g + 1)
            await_x(g + 1)
        collect(g)

    tally[0] = jnp.broadcast_to(picks_of(sibling), tally.shape[1:])
    swap = remote(tally.at[0], tally.at[1], tally_sem.at[0], tally_sem.at[1], sibling)
    pending.append(swap)
    count = picks_of(me)
    for g in range(batches):
        finish(g)
    arrived(tally.at[1], tally_sem.at[0], tally_sem.at[1])
    load_ref[...] = (count + tally[1, :1, :1]).astype(jnp.int32)
    for copy in pending:
        copy.wait_send()


def per_device(
    activations,
    pick_weight,
    expert_ids,
    replica,
    old_home,
    new_expert,
    gate_panel,
    up_panel,
    down_panel,
):
    n = lax.axis_size("expert")
    hi, lo = grid_of(n)
    batches, t, width = activations.shape
    half = gate_panel.shape[2]
    total = hi * lo * t
    dma = pltpu.SemaphoreType.DMA
    vmem = pl.BlockSpec(memory_space=pltpu.VMEM)
    hbm = pl.BlockSpec(memory_space=pl.ANY)
    bf16 = jnp.bfloat16
    out, load = pl.pallas_call(
        functools.partial(layer_kernel, hi, lo),
        out_shape=(
            jax.ShapeDtypeStruct(activations.shape, bf16),
            jax.ShapeDtypeStruct((1, 1), jnp.int32),
        ),
        in_specs=[hbm, vmem, vmem, vmem, vmem, vmem, hbm, hbm, hbm],
        out_specs=(vmem, vmem),
        scratch_shapes=[
            pltpu.VMEM((batches, total, width + LANES), bf16),
            pltpu.VMEM((width, 4 * half), bf16),
            pltpu.VMEM((width, 2 * half), bf16),
            pltpu.VMEM((batches, total, 2 * half), bf16),
            pltpu.VMEM((batches, total, width), bf16),
            pltpu.VMEM((batches, lo, hi, t, width), bf16),
            pltpu.VMEM((batches, hi, t, width), bf16),
            pltpu.VMEM((batches, hi, t, width), bf16),
            pltpu.VMEM((2, 8, LANES), jnp.float32),
            dma((batches + 3,)),
            dma((3,)),
            dma((3,)),
            dma((batches, hi)),
            dma((batches, hi)),
            dma((batches, hi, lo)),
            dma((batches, hi, lo)),
            dma((batches, hi, lo)),
            dma((batches, hi, lo)),
            dma((batches, hi)),
            dma((batches, hi)),
            dma((2,)),
        ],
        compiler_params=pltpu.CompilerParams(
            collective_id=0, has_side_effects=True, vmem_limit_bytes=60 * 1024 * 1024
        ),
        cost_estimate=pl.CostEstimate(
            flops=12 * batches * total * width * half,
            bytes_accessed=12 * width * half,
            transcendentals=2 * batches * total * half,
        ),
        name="expert_layer",
    )(
        activations,
        pick_weight.transpose(0, 2, 1),
        expert_ids.transpose(0, 2, 1),
        replica.transpose(0, 2, 1),
        old_home.reshape(1, -1),
        new_expert.reshape(1, -1),
        gate_panel,
        up_panel,
        down_panel,
    )
    return out, load.reshape(1)


def solution(mesh):
    return jax.shard_map(
        per_device,
        mesh=mesh,
        in_specs=(
            P(None, ("groups", "expert"), None),
            P(None, ("groups", "expert"), None),
            P(None, ("groups", "expert"), None),
            P(None, ("groups", "expert"), None),
            P(),
            P("groups"),
            P("expert", None, None),
            P("expert", None, None),
            P("expert", None, None),
        ),
        out_specs=(P(None, ("groups", "expert"), None), P(("groups", "expert"))),
        check_vma=False,
    )
```

```python
import functools
import math

import jax
import jax.numpy as jnp
from jax import lax
from jax.experimental import pallas as pl
from jax.experimental.pallas import tpu as pltpu
from jax.sharding import PartitionSpec as P

MESH = pl.DeviceIdType.MESH
LANES = 128
ROWS = 256


def grid_of(devices):
    chips = devices // 2
    lo = max(d for d in range(1, math.isqrt(chips) + 1) if chips % d == 0)
    return chips // lo, lo


def layer_kernel(
    hi,
    lo,
    act_ref,
    weight_ref,
    ids_ref,
    rep_ref,
    home_ref,
    row_ref,
    gate_ref,
    up_ref,
    down_ref,
    out_ref,
    load_ref,
    tok,
    wgu,
    wd,
    hid,
    res,
    xbuf,
    comb,
    fin,
    tally,
    local_sem,
    panel_send,
    panel_recv,
    z_send,
    z_recv,
    x_send,
    x_recv,
    rx_send,
    rx_recv,
    rz_send,
    rz_recv,
    tally_sem,
):
    batches, t, width = act_ref.shape
    top = ids_ref.shape[1]
    half = gate_ref.shape[2]
    full = 2 * half
    me = lax.axis_index("expert")
    core = lax.rem(me, 2)
    chip = me // 2
    xi = lax.rem(chip, lo)
    zi = chip // lo
    sibling = chip * 2 + (1 - core)

    def chip_at(dz, dx):
        z = lax.rem(zi + dz + hi, hi)
        x = lax.rem(xi + dx + lo, lo)
        return z * lo + x

    def device_at(dz, dx):
        return chip_at(dz, dx) * 2 + core

    def rows(place):
        return pl.ds(pl.multiple_of(place * t, t), t)

    def remote(src, dst, send, recv, device):
        copy = pltpu.make_async_remote_copy(
            src_ref=src,
            dst_ref=dst,
            send_sem=send,
            recv_sem=recv,
            device_id={"expert": device},
            device_id_type=MESH,
        )
        copy.start()
        return copy

    def arrived(ref, send, recv):
        pltpu.make_async_remote_copy(
            src_ref=ref,
            dst_ref=ref,
            send_sem=send,
            recv_sem=recv,
            device_id={"expert": sibling},
            device_id_type=MESH,
        ).wait_recv()

    def local(src, dst, sem):
        copy = pltpu.make_async_copy(src, dst, sem)
        copy.start()
        return copy

    peers = [device_at(dz, 0) for dz in range(1, hi)]
    peers += [device_at(0, dx) for dx in range(1, lo)] + [sibling]
    barrier = pltpu.get_barrier_semaphore()
    for peer in peers:
        pl.semaphore_signal(barrier, inc=1, device_id={"expert": peer}, device_id_type=MESH)

    gate_cols = pl.ds(pl.multiple_of(core * half, LANES), half)
    up_cols = pl.ds(pl.multiple_of(full + core * half, LANES), half)
    panels = (
        (gate_ref.at[0], wgu.at[:, gate_cols]),
        (up_ref.at[0], wgu.at[:, up_cols]),
        (down_ref.at[0], wd.at[:, gate_cols]),
    )
    act_copies = [
        local(act_ref.at[g], tok.at[g, rows(chip), pl.ds(0, width)], local_sem.at[g])
        for g in range(batches)
    ]
    panel_copies = [
        local(src, dst, local_sem.at[batches + p]) for p, (src, dst) in enumerate(panels)
    ]

    def upright(line):
        count = line.shape[1]
        shape = (count, count)
        same = lax.broadcasted_iota(jnp.int32, shape, 0) == lax.broadcasted_iota(
            jnp.int32, shape, 1
        )
        return jnp.sum(jnp.where(same, line, jnp.zeros_like(line)), axis=1, keepdims=True)

    row = row_ref[...]
    slots = row.shape[1]
    s_lane = lax.broadcasted_iota(jnp.int32, (slots, slots), 1)
    s_row = lax.broadcasted_iota(jnp.int32, (slots, slots), 0)
    earlier = (upright(row) == row) & (s_row < s_lane)
    ranks = jnp.sum(earlier.astype(jnp.int32), axis=0, keepdims=True)
    homes = home_ref[...]
    lane_slot = lax.broadcasted_iota(jnp.int32, (t, slots), 1)
    lane_expert = lax.broadcasted_iota(jnp.int32, (t, homes.shape[1]), 1)
    lane = lax.broadcasted_iota(jnp.int32, (t, LANES), 1)
    for g in range(batches):
        marks = jnp.zeros((t, LANES), jnp.float32)
        for k in range(top):
            ids = upright(ids_ref[g, k : k + 1, :])
            rep = upright(rep_ref[g, k : k + 1, :])
            weight = upright(weight_ref[g, k : k + 1, :])
            home = jnp.sum(jnp.where(lane_expert == ids, homes, 0), axis=1, keepdims=True)
            match = (row == ids) & (ranks == rep)
            slot = jnp.sum(jnp.where(match, lane_slot, 0), axis=1, keepdims=True)
            first = weight.astype(jnp.bfloat16).astype(jnp.float32)
            second = (weight - first).astype(jnp.bfloat16).astype(jnp.float32)
            third = weight - first - second
            parts = (home.astype(jnp.float32), slot.astype(jnp.float32), first, second, third)
            for place, part in enumerate(parts):
                marks = jnp.where(lane == place * top + k, part, marks)
        tok[g, rows(chip), pl.ds(width, LANES)] = marks.astype(jnp.bfloat16)

    pl.semaphore_wait(barrier, len(peers))

    pending = []

    moves = [(2 * s - (sign < 0), sign, s) for s in range(1, hi) for sign in (-1, 1)]

    def present(sign, s):
        return zi >= s if sign < 0 else zi + s < hi

    def onward(sign):
        return zi + 1 < hi if sign < 0 else zi >= 1

    def across(g, place, block):
        return [
            remote(
                block, block, x_send.at[g, place, dx], x_recv.at[g, place, dx], device_at(0, dx)
            )
            for dx in range(1, lo)
        ]

    def send_on(g, block, sign, s):
        place = 2 * s - (sign < 0)

        @pl.when(onward(sign))
        def _():
            remote(
                block,
                block,
                z_send.at[g, place],
                z_recv.at[g, place],
                device_at(-sign, 0),
            )

    def send_z(g):
        act_copies[g].wait()
        block = tok.at[g, rows(chip)]
        for sign in (-1, 1):
            send_on(g, block, sign, 1)
        across(g, 0, block)

    def relay_z(g):
        for place, sign, s in moves:

            @pl.when(present(sign, s))
            def _():
                block = tok.at[g, rows((zi + sign * s) * lo + xi)]
                arrived(block, z_send.at[g, place], z_recv.at[g, place])
                if s + 1 < hi:
                    send_on(g, block, sign, s + 1)
                across(g, place, block)

    def await_x(g):
        for dx in range(1, lo):
            x = lax.rem(xi + lo - dx, lo)
            arrived(tok.at[g, rows(zi * lo + x)], x_send.at[g, 0, dx], x_recv.at[g, 0, dx])
        for place, sign, s in moves:

            @pl.when(present(sign, s))
            def _():
                for dx in range(1, lo):
                    x = lax.rem(xi + lo - dx, lo)
                    arrived(
                        tok.at[g, rows((zi + sign * s) * lo + x)],
                        x_send.at[g, place, dx],
                        x_recv.at[g, place, dx],
                    )

    def sent(ref, send, recv):
        pltpu.make_async_remote_copy(
            src_ref=ref,
            dst_ref=ref,
            send_sem=send,
            recv_sem=recv,
            device_id={"expert": sibling},
            device_id_type=MESH,
        ).wait_send()

    def await_sent(g):
        block = tok.at[g, rows(chip)]
        for dx in range(1, lo):
            sent(block, x_send.at[g, 0, dx], x_recv.at[g, 0, dx])
        for place, sign, s in moves:

            @pl.when(present(sign, s))
            def _():
                for dx in range(1, lo):
                    sent(block, x_send.at[g, place, dx], x_recv.at[g, place, dx])

            @pl.when(present(sign, s - 1) & onward(sign))
            def _():
                sent(block, z_send.at[g, place], z_recv.at[g, place])

    total = hi * lo * t
    step = min(ROWS, total)

    def chunks(body):
        if total == step:
            body(pl.ds(0, step))
        else:

            @pl.loop(0, total // step)
            def _(i):
                body(pl.ds(pl.multiple_of(i * step, step), step))

    def hidden(g):
        def body(part):
            both = jnp.dot(
                tok[g, part, pl.ds(0, width)], wgu[...], preferred_element_type=jnp.float32
            )
            gate, up = both[:, :full], both[:, full:]
            hid[g, part, :] = (gate / (1.0 + jnp.exp(-gate)) * up).astype(jnp.bfloat16)

        chunks(body)

    def result(g):
        def body(part):
            value = lax.dot_general(
                hid[g, part, :],
                wd[...],
                (((1,), (1,)), ((), ())),
                preferred_element_type=jnp.float32,
            )
            value = value.astype(jnp.bfloat16).astype(jnp.float32)
            marks = tok[g, part, pl.ds(width, LANES)].astype(jnp.float32)
            scale = jnp.zeros((step, 1), jnp.float32)
            for k in range(top):
                home, _, first, second, third = (
                    marks[:, p * top + k : p * top + k + 1] for p in range(5)
                )
                weight = first + (second + third)
                scale += jnp.where(home == chip.astype(jnp.float32), weight, 0.0)
            res[g, part, :] = (value * scale).astype(jnp.bfloat16)

        chunks(body)
        for dz in back_order:
            for dx in range(1, lo):
                pending.append(
                    remote(
                        res.at[g, rows(chip_at(dz, dx))],
                        xbuf.at[g, dx, dz],
                        rx_send.at[g, dz, dx],
                        rx_recv.at[g, dz, dx],
                        device_at(0, dx),
                    )
                )

    back_order = list(range(1, hi)) + [0]

    def collect(g):
        for dz in back_order:
            value = res[g, rows(chip_at(dz, 0)), :].astype(jnp.float32)
            for dx in range(1, lo):
                arrived(xbuf.at[g, dx, dz], rx_send.at[g, dz, dx], rx_recv.at[g, dz, dx])
                value += xbuf[g, dx, dz].astype(jnp.float32)
            if dz:
                comb[g, dz] = value.astype(jnp.bfloat16)
                pending.append(
                    remote(
                        comb.at[g, dz],
                        fin.at[g, dz],
                        rz_send.at[g, dz],
                        rz_recv.at[g, dz],
                        device_at(dz, 0),
                    )
                )
            else:
                fin[g, 0] = value.astype(jnp.bfloat16)

    def finish(g):
        value = fin[g, 0].astype(jnp.float32)
        for dz in range(1, hi):
            arrived(fin.at[g, dz], rz_send.at[g, dz], rz_recv.at[g, dz])
            value += fin[g, dz].astype(jnp.float32)
        out_ref[g] = value.astype(jnp.bfloat16)

    def await_panel(p):
        panel_copies[p].wait()
        first = pl.multiple_of((1 - core) * half, LANES)
        if p == 0:
            ref = wgu.at[:, pl.ds(first, half)]
        elif p == 1:
            ref = wgu.at[:, pl.ds(pl.multiple_of(full + first, LANES), half)]
        else:
            ref = wd.at[:, pl.ds(first, half)]
        arrived(ref, panel_send.at[p], panel_recv.at[p])

    def picks_of(slot):
        count = jnp.zeros((1, 1), jnp.float32)
        for g in range(batches):
            marks = tok[g, :, pl.ds(width, LANES)].astype(jnp.float32)
            place = lax.broadcasted_iota(jnp.int32, marks.shape, 1)
            mine = (place >= top) & (place < 2 * top) & (marks == slot.astype(jnp.float32))
            per_lane = jnp.sum(jnp.where(mine, 1.0, 0.0), axis=0, keepdims=True)
            count += jnp.sum(per_lane, axis=1, keepdims=True)
        return count

    send_z(0)
    pushed = [
        remote(src, dst, panel_send.at[p], panel_recv.at[p], sibling)
        for p, (src, dst) in enumerate(panels)
    ]
    pending.extend(pushed)
    relay_z(0)
    for g in range(1, batches):
        send_z(g)
    await_x(0)
    for g in range(batches):
        if g == 0:
            await_panel(0)
            await_panel(1)
        hidden(g)
        if g == 0:
            await_panel(2)
        result(g)
        if g + 1 < batches:
            relay_z(g + 1)
            await_x(g + 1)
        collect(g)

    tally[0] = jnp.broadcast_to(picks_of(sibling), tally.shape[1:])
    swap = remote(tally.at[0], tally.at[1], tally_sem.at[0], tally_sem.at[1], sibling)
    pending.append(swap)
    count = picks_of(me)
    for g in range(batches):
        finish(g)
    arrived(tally.at[1], tally_sem.at[0], tally_sem.at[1])
    load_ref[...] = (count + tally[1, :1, :1]).astype(jnp.int32)
    for g in range(batches):
        await_sent(g)
    for copy in pending:
        copy.wait_send()


def per_device(
    activations,
    pick_weight,
    expert_ids,
    replica,
    old_home,
    new_expert,
    gate_panel,
    up_panel,
    down_panel,
):
    n = lax.axis_size("expert")
    hi, lo = grid_of(n)
    batches, t, width = activations.shape
    half = gate_panel.shape[2]
    total = hi * lo * t
    dma = pltpu.SemaphoreType.DMA
    vmem = pl.BlockSpec(memory_space=pltpu.VMEM)
    hbm = pl.BlockSpec(memory_space=pl.ANY)
    bf16 = jnp.bfloat16
    out, load = pl.pallas_call(
        functools.partial(layer_kernel, hi, lo),
        out_shape=(
            jax.ShapeDtypeStruct(activations.shape, bf16),
            jax.ShapeDtypeStruct((1, 1), jnp.int32),
        ),
        in_specs=[hbm, vmem, vmem, vmem, vmem, vmem, hbm, hbm, hbm],
        out_specs=(vmem, vmem),
        scratch_shapes=[
            pltpu.VMEM((batches, total, width + LANES), bf16),
            pltpu.VMEM((width, 4 * half), bf16),
            pltpu.VMEM((width, 2 * half), bf16),
            pltpu.VMEM((batches, total, 2 * half), bf16),
            pltpu.VMEM((batches, total, width), bf16),
            pltpu.VMEM((batches, lo, hi, t, width), bf16),
            pltpu.VMEM((batches, hi, t, width), bf16),
            pltpu.VMEM((batches, hi, t, width), bf16),
            pltpu.VMEM((2, 8, LANES), jnp.float32),
            dma((batches + 3,)),
            dma((3,)),
            dma((3,)),
            dma((batches, 2 * hi - 1)),
            dma((batches, 2 * hi - 1)),
            dma((batches, 2 * hi - 1, lo)),
            dma((batches, 2 * hi - 1, lo)),
            dma((batches, hi, lo)),
            dma((batches, hi, lo)),
            dma((batches, hi)),
            dma((batches, hi)),
            dma((2,)),
        ],
        compiler_params=pltpu.CompilerParams(
            collective_id=0, has_side_effects=True, vmem_limit_bytes=60 * 1024 * 1024
        ),
        cost_estimate=pl.CostEstimate(
            flops=12 * batches * total * width * half,
            bytes_accessed=12 * width * half,
            transcendentals=2 * batches * total * half,
        ),
        name="expert_layer",
    )(
        activations,
        pick_weight.transpose(0, 2, 1),
        expert_ids.transpose(0, 2, 1),
        replica.transpose(0, 2, 1),
        old_home.reshape(1, -1),
        new_expert.reshape(1, -1),
        gate_panel,
        up_panel,
        down_panel,
    )
    return out, load.reshape(1)


def solution(mesh):
    return jax.shard_map(
        per_device,
        mesh=mesh,
        in_specs=(
            P(None, ("groups", "expert"), None),
            P(None, ("groups", "expert"), None),
            P(None, ("groups", "expert"), None),
            P(None, ("groups", "expert"), None),
            P(),
            P("groups"),
            P("expert", None, None),
            P("expert", None, None),
            P("expert", None, None),
        ),
        out_specs=(P(None, ("groups", "expert"), None), P(("groups", "expert"))),
        check_vma=False,
    )
```

```python
import functools
import math

import jax
import jax.numpy as jnp
from jax import lax
from jax.experimental import pallas as pl
from jax.experimental.pallas import tpu as pltpu
from jax.sharding import PartitionSpec as P

MESH = pl.DeviceIdType.MESH
LANES = 128
ROWS = 256
PARTS = 4


def grid_of(devices):
    chips = devices // 2
    lo = max(d for d in range(1, math.isqrt(chips) + 1) if chips % d == 0)
    return chips // lo, lo


def layer_kernel(
    hi,
    lo,
    act_ref,
    weight_ref,
    ids_ref,
    rep_ref,
    home_ref,
    row_ref,
    gate_ref,
    up_ref,
    down_ref,
    out_ref,
    load_ref,
    tok,
    wgu,
    wd,
    hid,
    res,
    xbuf,
    comb,
    fin,
    tally,
    local_sem,
    panel_send,
    panel_recv,
    z_send,
    z_recv,
    x_send,
    x_recv,
    rx_send,
    rx_recv,
    rz_send,
    rz_recv,
    tally_sem,
):
    batches, t, width = act_ref.shape
    top = ids_ref.shape[1]
    half = gate_ref.shape[2]
    full = 2 * half
    piece = width // PARTS
    me = lax.axis_index("expert")
    core = lax.rem(me, 2)
    chip = me // 2
    xi = lax.rem(chip, lo)
    zi = chip // lo
    sibling = chip * 2 + (1 - core)

    def chip_at(dz, dx):
        z = lax.rem(zi + dz + hi, hi)
        x = lax.rem(xi + dx + lo, lo)
        return z * lo + x

    def device_at(dz, dx):
        return chip_at(dz, dx) * 2 + core

    def rows(place):
        return pl.ds(pl.multiple_of(place * t, t), t)

    def remote(src, dst, send, recv, device):
        copy = pltpu.make_async_remote_copy(
            src_ref=src,
            dst_ref=dst,
            send_sem=send,
            recv_sem=recv,
            device_id={"expert": device},
            device_id_type=MESH,
        )
        copy.start()
        return copy

    def arrived(ref, send, recv):
        pltpu.make_async_remote_copy(
            src_ref=ref,
            dst_ref=ref,
            send_sem=send,
            recv_sem=recv,
            device_id={"expert": sibling},
            device_id_type=MESH,
        ).wait_recv()

    def local(src, dst, sem):
        copy = pltpu.make_async_copy(src, dst, sem)
        copy.start()
        return copy

    peers = [device_at(dz, 0) for dz in range(1, hi)]
    peers += [device_at(0, dx) for dx in range(1, lo)] + [sibling]
    barrier = pltpu.get_barrier_semaphore()
    for peer in peers:
        pl.semaphore_signal(barrier, inc=1, device_id={"expert": peer}, device_id_type=MESH)

    gate_cols = pl.ds(pl.multiple_of(core * half, LANES), half)
    up_cols = pl.ds(pl.multiple_of(full + core * half, LANES), half)
    panels = (
        (gate_ref.at[0], wgu.at[:, gate_cols]),
        (up_ref.at[0], wgu.at[:, up_cols]),
        (down_ref.at[0], wd.at[:, gate_cols]),
    )
    act_copies = [
        local(act_ref.at[g], tok.at[g, rows(chip), pl.ds(0, width)], local_sem.at[g])
        for g in range(batches)
    ]
    panel_copies = [
        local(src, dst, local_sem.at[batches + p]) for p, (src, dst) in enumerate(panels)
    ]

    def upright(line):
        count = line.shape[1]
        shape = (count, count)
        same = lax.broadcasted_iota(jnp.int32, shape, 0) == lax.broadcasted_iota(
            jnp.int32, shape, 1
        )
        return jnp.sum(jnp.where(same, line, jnp.zeros_like(line)), axis=1, keepdims=True)

    row = row_ref[...]
    slots = row.shape[1]
    s_lane = lax.broadcasted_iota(jnp.int32, (slots, slots), 1)
    s_row = lax.broadcasted_iota(jnp.int32, (slots, slots), 0)
    earlier = (upright(row) == row) & (s_row < s_lane)
    ranks = jnp.sum(earlier.astype(jnp.int32), axis=0, keepdims=True)
    homes = home_ref[...]
    lane_slot = lax.broadcasted_iota(jnp.int32, (t, slots), 1)
    lane_expert = lax.broadcasted_iota(jnp.int32, (t, homes.shape[1]), 1)
    lane = lax.broadcasted_iota(jnp.int32, (t, LANES), 1)
    for g in range(batches):
        marks = jnp.zeros((t, LANES), jnp.float32)
        for k in range(top):
            ids = upright(ids_ref[g, k : k + 1, :])
            rep = upright(rep_ref[g, k : k + 1, :])
            weight = upright(weight_ref[g, k : k + 1, :])
            home = jnp.sum(jnp.where(lane_expert == ids, homes, 0), axis=1, keepdims=True)
            match = (row == ids) & (ranks == rep)
            slot = jnp.sum(jnp.where(match, lane_slot, 0), axis=1, keepdims=True)
            first = weight.astype(jnp.bfloat16).astype(jnp.float32)
            second = (weight - first).astype(jnp.bfloat16).astype(jnp.float32)
            third = weight - first - second
            parts = (home.astype(jnp.float32), slot.astype(jnp.float32), first, second, third)
            for place, part in enumerate(parts):
                marks = jnp.where(lane == place * top + k, part, marks)
        tok[g, rows(chip), pl.ds(width, LANES)] = marks.astype(jnp.bfloat16)

    pl.semaphore_wait(barrier, len(peers))

    pending = []

    def across(g, dz):
        block = tok.at[g, rows(chip_at(-dz, 0))]
        for dx in range(1, lo):
            pending.append(
                remote(
                    block, block, x_send.at[g, dz, dx], x_recv.at[g, dz, dx], device_at(0, dx)
                )
            )

    def send_z(g):
        act_copies[g].wait()
        block = tok.at[g, rows(chip)]
        for dz in range(1, hi):
            pending.append(
                remote(block, block, z_send.at[g, dz], z_recv.at[g, dz], device_at(dz, 0))
            )
        across(g, 0)

    def relay_z(g):
        for dz in range(1, hi):
            arrived(tok.at[g, rows(chip_at(-dz, 0))], z_send.at[g, dz], z_recv.at[g, dz])
            across(g, dz)

    def await_x(g):
        for dz in range(hi):
            for dx in range(1, lo):
                arrived(
                    tok.at[g, rows(chip_at(-dz, -dx))],
                    x_send.at[g, dz, dx],
                    x_recv.at[g, dz, dx],
                )

    total = hi * lo * t
    step = min(ROWS, total)

    def chunks(body):
        if total == step:
            body(pl.ds(0, step))
        else:

            @pl.loop(0, total // step)
            def _(i):
                body(pl.ds(pl.multiple_of(i * step, step), step))

    def hidden(g):
        def body(part):
            both = jnp.dot(
                tok[g, part, pl.ds(0, width)], wgu[...], preferred_element_type=jnp.float32
            )
            gate, up = both[:, :full], both[:, full:]
            hid[g, part, :] = (gate / (1.0 + jnp.exp(-gate)) * up).astype(jnp.bfloat16)

        chunks(body)

    def result(g):
        def body(part):
            value = lax.dot_general(
                hid[g, part, :],
                wd[...],
                (((1,), (1,)), ((), ())),
                preferred_element_type=jnp.float32,
            )
            value = value.astype(jnp.bfloat16).astype(jnp.float32)
            marks = tok[g, part, pl.ds(width, LANES)].astype(jnp.float32)
            scale = jnp.zeros((step, 1), jnp.float32)
            for k in range(top):
                home, _, first, second, third = (
                    marks[:, p * top + k : p * top + k + 1] for p in range(5)
                )
                weight = first + (second + third)
                scale += jnp.where(home == chip.astype(jnp.float32), weight, 0.0)
            res[g, part, :] = (value * scale).astype(jnp.bfloat16)

        chunks(body)
        for dz in back_order:
            for dx in range(1, lo):
                pending.append(
                    remote(
                        res.at[g, rows(chip_at(dz, dx))],
                        xbuf.at[g, dx, dz],
                        rx_send.at[g, dz, dx],
                        rx_recv.at[g, dz, dx],
                        device_at(0, dx),
                    )
                )

    back_order = list(range(1, hi)) + [0]

    def collect(g):
        for dz in back_order:
            value = res[g, rows(chip_at(dz, 0)), :].astype(jnp.float32)
            for dx in range(1, lo):
                arrived(xbuf.at[g, dx, dz], rx_send.at[g, dz, dx], rx_recv.at[g, dz, dx])
                value += xbuf[g, dx, dz].astype(jnp.float32)
            if dz:
                comb[g, dz] = value.astype(jnp.bfloat16)
                pending.append(
                    remote(
                        comb.at[g, dz],
                        fin.at[g, dz],
                        rz_send.at[g, dz],
                        rz_recv.at[g, dz],
                        device_at(dz, 0),
                    )
                )
            else:
                fin[g, 0] = value.astype(jnp.bfloat16)

    def finish(g):
        value = fin[g, 0].astype(jnp.float32)
        for dz in range(1, hi):
            arrived(fin.at[g, dz], rz_send.at[g, dz], rz_recv.at[g, dz])
            value += fin[g, dz].astype(jnp.float32)
        out_ref[g] = value.astype(jnp.bfloat16)

    def await_panel(p):
        panel_copies[p].wait()
        first = pl.multiple_of((1 - core) * half, LANES)
        if p == 0:
            ref = wgu.at[:, pl.ds(first, half)]
        elif p == 1:
            ref = wgu.at[:, pl.ds(pl.multiple_of(full + first, LANES), half)]
        else:
            ref = wd.at[:, pl.ds(first, half)]
        for q in range(PARTS):
            arrived(ref.at[pl.ds(q * piece, piece)], panel_send.at[p, q], panel_recv.at[p, q])

    def picks_of(slot):
        count = jnp.zeros((1, 1), jnp.float32)
        for g in range(batches):
            marks = tok[g, :, pl.ds(width, LANES)].astype(jnp.float32)
            place = lax.broadcasted_iota(jnp.int32, marks.shape, 1)
            mine = (place >= top) & (place < 2 * top) & (marks == slot.astype(jnp.float32))
            per_lane = jnp.sum(jnp.where(mine, 1.0, 0.0), axis=0, keepdims=True)
            count += jnp.sum(per_lane, axis=1, keepdims=True)
        return count

    send_z(0)
    for p, (src, dst) in enumerate(panels):
        for q in range(PARTS):
            part = pl.ds(q * piece, piece)
            pending.append(
                remote(
                    src.at[part],
                    dst.at[part],
                    panel_send.at[p, q],
                    panel_recv.at[p, q],
                    sibling,
                )
            )
    relay_z(0)
    for g in range(1, batches):
        send_z(g)
    await_x(0)
    for g in range(batches):
        if g == 0:
            await_panel(0)
            await_panel(1)
        hidden(g)
        if g == 0:
            await_panel(2)
        result(g)
        if g + 1 < batches:
            relay_z(g + 1)
            await_x(g + 1)
        collect(g)

    tally[0] = jnp.broadcast_to(picks_of(sibling), tally.shape[1:])
    swap = remote(tally.at[0], tally.at[1], tally_sem.at[0], tally_sem.at[1], sibling)
    pending.append(swap)
    count = picks_of(me)
    for g in range(batches):
        finish(g)
    arrived(tally.at[1], tally_sem.at[0], tally_sem.at[1])
    load_ref[...] = (count + tally[1, :1, :1]).astype(jnp.int32)
    for copy in pending:
        copy.wait_send()


def per_device(
    activations,
    pick_weight,
    expert_ids,
    replica,
    old_home,
    new_expert,
    gate_panel,
    up_panel,
    down_panel,
):
    n = lax.axis_size("expert")
    hi, lo = grid_of(n)
    batches, t, width = activations.shape
    half = gate_panel.shape[2]
    total = hi * lo * t
    dma = pltpu.SemaphoreType.DMA
    vmem = pl.BlockSpec(memory_space=pltpu.VMEM)
    hbm = pl.BlockSpec(memory_space=pl.ANY)
    bf16 = jnp.bfloat16
    out, load = pl.pallas_call(
        functools.partial(layer_kernel, hi, lo),
        out_shape=(
            jax.ShapeDtypeStruct(activations.shape, bf16),
            jax.ShapeDtypeStruct((1, 1), jnp.int32),
        ),
        in_specs=[hbm, vmem, vmem, vmem, vmem, vmem, hbm, hbm, hbm],
        out_specs=(vmem, vmem),
        scratch_shapes=[
            pltpu.VMEM((batches, total, width + LANES), bf16),
            pltpu.VMEM((width, 4 * half), bf16),
            pltpu.VMEM((width, 2 * half), bf16),
            pltpu.VMEM((batches, total, 2 * half), bf16),
            pltpu.VMEM((batches, total, width), bf16),
            pltpu.VMEM((batches, lo, hi, t, width), bf16),
            pltpu.VMEM((batches, hi, t, width), bf16),
            pltpu.VMEM((batches, hi, t, width), bf16),
            pltpu.VMEM((2, 8, LANES), jnp.float32),
            dma((batches + 3,)),
            dma((3, PARTS)),
            dma((3, PARTS)),
            dma((batches, hi)),
            dma((batches, hi)),
            dma((batches, hi, lo)),
            dma((batches, hi, lo)),
            dma((batches, hi, lo)),
            dma((batches, hi, lo)),
            dma((batches, hi)),
            dma((batches, hi)),
            dma((2,)),
        ],
        compiler_params=pltpu.CompilerParams(
            collective_id=0, has_side_effects=True, vmem_limit_bytes=60 * 1024 * 1024
        ),
        cost_estimate=pl.CostEstimate(
            flops=12 * batches * total * width * half,
            bytes_accessed=12 * width * half,
            transcendentals=2 * batches * total * half,
        ),
        name="expert_layer",
    )(
        activations,
        pick_weight.transpose(0, 2, 1),
        expert_ids.transpose(0, 2, 1),
        replica.transpose(0, 2, 1),
        old_home.reshape(1, -1),
        new_expert.reshape(1, -1),
        gate_panel,
        up_panel,
        down_panel,
    )
    return out, load.reshape(1)


def solution(mesh):
    return jax.shard_map(
        per_device,
        mesh=mesh,
        in_specs=(
            P(None, ("groups", "expert"), None),
            P(None, ("groups", "expert"), None),
            P(None, ("groups", "expert"), None),
            P(None, ("groups", "expert"), None),
            P(),
            P("groups"),
            P("expert", None, None),
            P("expert", None, None),
            P("expert", None, None),
        ),
        out_specs=(P(None, ("groups", "expert"), None), P(("groups", "expert"))),
        check_vma=False,
    )
```

```python
import functools
import math

import jax
import jax.numpy as jnp
from jax import lax
from jax.experimental import pallas as pl
from jax.experimental.pallas import tpu as pltpu
from jax.sharding import PartitionSpec as P

MESH = pl.DeviceIdType.MESH
LANES = 128
ROWS = 256
PARTS = 4


def grid_of(devices):
    chips = devices // 2
    lo = max(d for d in range(1, math.isqrt(chips) + 1) if chips % d == 0)
    return chips // lo, lo


def layer_kernel(
    hi,
    lo,
    act_ref,
    weight_ref,
    ids_ref,
    rep_ref,
    home_ref,
    row_ref,
    gate_ref,
    up_ref,
    down_ref,
    out_ref,
    load_ref,
    tok,
    wgu,
    wd,
    stage,
    hid,
    res,
    xbuf,
    comb,
    fin,
    tally,
    local_sem,
    panel_send,
    panel_recv,
    z_send,
    z_recv,
    x_send,
    x_recv,
    rx_send,
    rx_recv,
    rz_send,
    rz_recv,
    tally_sem,
):
    batches, t, width = act_ref.shape
    top = ids_ref.shape[1]
    half = gate_ref.shape[2]
    full = 2 * half
    piece = width // PARTS
    me = lax.axis_index("expert")
    core = lax.rem(me, 2)
    chip = me // 2
    xi = lax.rem(chip, lo)
    zi = chip // lo
    sibling = chip * 2 + (1 - core)

    def chip_at(dz, dx):
        z = lax.rem(zi + dz + hi, hi)
        x = lax.rem(xi + dx + lo, lo)
        return z * lo + x

    def device_at(dz, dx):
        return chip_at(dz, dx) * 2 + core

    def rows(place):
        return pl.ds(pl.multiple_of(place * t, t), t)

    def remote(src, dst, send, recv, device):
        copy = pltpu.make_async_remote_copy(
            src_ref=src,
            dst_ref=dst,
            send_sem=send,
            recv_sem=recv,
            device_id={"expert": device},
            device_id_type=MESH,
        )
        copy.start()
        return copy

    def arrived(ref, send, recv):
        pltpu.make_async_remote_copy(
            src_ref=ref,
            dst_ref=ref,
            send_sem=send,
            recv_sem=recv,
            device_id={"expert": sibling},
            device_id_type=MESH,
        ).wait_recv()

    def local(src, dst, sem):
        copy = pltpu.make_async_copy(src, dst, sem)
        copy.start()
        return copy

    peers = [device_at(dz, 0) for dz in range(1, hi)]
    peers += [device_at(0, dx) for dx in range(1, lo)] + [sibling]
    barrier = pltpu.get_barrier_semaphore()
    for peer in peers:
        pl.semaphore_signal(barrier, inc=1, device_id={"expert": peer}, device_id_type=MESH)

    gate_cols = pl.ds(pl.multiple_of(core * half, LANES), half)
    up_cols = pl.ds(pl.multiple_of(full + core * half, LANES), half)
    panels = (
        (gate_ref.at[0], wgu.at[:, gate_cols]),
        (up_ref.at[0], wgu.at[:, up_cols]),
        (down_ref.at[0], stage),
    )
    act_copies = [
        local(act_ref.at[g], tok.at[g, rows(chip), pl.ds(0, width)], local_sem.at[g])
        for g in range(batches)
    ]
    panel_copies = [
        local(src, dst, local_sem.at[batches + p]) for p, (src, dst) in enumerate(panels)
    ]

    def upright(line):
        count = line.shape[1]
        shape = (count, count)
        same = lax.broadcasted_iota(jnp.int32, shape, 0) == lax.broadcasted_iota(
            jnp.int32, shape, 1
        )
        return jnp.sum(jnp.where(same, line, jnp.zeros_like(line)), axis=1, keepdims=True)

    row = row_ref[...]
    slots = row.shape[1]
    s_lane = lax.broadcasted_iota(jnp.int32, (slots, slots), 1)
    s_row = lax.broadcasted_iota(jnp.int32, (slots, slots), 0)
    earlier = (upright(row) == row) & (s_row < s_lane)
    ranks = jnp.sum(earlier.astype(jnp.int32), axis=0, keepdims=True)
    homes = home_ref[...]
    lane_slot = lax.broadcasted_iota(jnp.int32, (t, slots), 1)
    lane_expert = lax.broadcasted_iota(jnp.int32, (t, homes.shape[1]), 1)
    lane = lax.broadcasted_iota(jnp.int32, (t, LANES), 1)
    for g in range(batches):
        marks = jnp.zeros((t, LANES), jnp.float32)
        for k in range(top):
            ids = upright(ids_ref[g, k : k + 1, :])
            rep = upright(rep_ref[g, k : k + 1, :])
            weight = upright(weight_ref[g, k : k + 1, :])
            home = jnp.sum(jnp.where(lane_expert == ids, homes, 0), axis=1, keepdims=True)
            match = (row == ids) & (ranks == rep)
            slot = jnp.sum(jnp.where(match, lane_slot, 0), axis=1, keepdims=True)
            first = weight.astype(jnp.bfloat16).astype(jnp.float32)
            second = (weight - first).astype(jnp.bfloat16).astype(jnp.float32)
            third = weight - first - second
            parts = (home.astype(jnp.float32), slot.astype(jnp.float32), first, second, third)
            for place, part in enumerate(parts):
                marks = jnp.where(lane == place * top + k, part, marks)
        tok[g, rows(chip), pl.ds(width, LANES)] = marks.astype(jnp.bfloat16)

    pl.semaphore_wait(barrier, len(peers))

    pending = []

    def across(g, dz):
        block = tok.at[g, rows(chip_at(-dz, 0))]
        for dx in range(1, lo):
            pending.append(
                remote(
                    block, block, x_send.at[g, dz, dx], x_recv.at[g, dz, dx], device_at(0, dx)
                )
            )

    def send_z(g):
        act_copies[g].wait()
        block = tok.at[g, rows(chip)]
        for dz in range(1, hi):
            pending.append(
                remote(block, block, z_send.at[g, dz], z_recv.at[g, dz], device_at(dz, 0))
            )
        across(g, 0)

    def relay_z(g):
        for dz in range(1, hi):
            arrived(tok.at[g, rows(chip_at(-dz, 0))], z_send.at[g, dz], z_recv.at[g, dz])
            across(g, dz)

    def await_x(g):
        for dz in range(hi):
            for dx in range(1, lo):
                arrived(
                    tok.at[g, rows(chip_at(-dz, -dx))],
                    x_send.at[g, dz, dx],
                    x_recv.at[g, dz, dx],
                )

    total = hi * lo * t
    step = min(ROWS, total)

    def chunks(body):
        if total == step:
            body(pl.ds(0, step))
        else:

            @pl.loop(0, total // step)
            def _(i):
                body(pl.ds(pl.multiple_of(i * step, step), step))

    def hidden(g):
        def body(part):
            both = jnp.dot(
                tok[g, part, pl.ds(0, width)], wgu[...], preferred_element_type=jnp.float32
            )
            gate, up = both[:, :full], both[:, full:]
            hid[g, part, :] = (gate / (1.0 + jnp.exp(-gate)) * up).astype(jnp.bfloat16)

        chunks(body)

    def result(g):
        def body(part):
            value = jnp.dot(hid[g, part, :], wd[...], preferred_element_type=jnp.float32)
            value = value.astype(jnp.bfloat16).astype(jnp.float32)
            marks = tok[g, part, pl.ds(width, LANES)].astype(jnp.float32)
            scale = jnp.zeros((step, 1), jnp.float32)
            for k in range(top):
                home, _, first, second, third = (
                    marks[:, p * top + k : p * top + k + 1] for p in range(5)
                )
                weight = first + (second + third)
                scale += jnp.where(home == chip.astype(jnp.float32), weight, 0.0)
            res[g, part, :] = (value * scale).astype(jnp.bfloat16)

        chunks(body)
        for dz in back_order:
            for dx in range(1, lo):
                pending.append(
                    remote(
                        res.at[g, rows(chip_at(dz, dx))],
                        xbuf.at[g, dx, dz],
                        rx_send.at[g, dz, dx],
                        rx_recv.at[g, dz, dx],
                        device_at(0, dx),
                    )
                )

    back_order = list(range(1, hi)) + [0]

    def collect(g):
        for dz in back_order:
            value = res[g, rows(chip_at(dz, 0)), :].astype(jnp.float32)
            for dx in range(1, lo):
                arrived(xbuf.at[g, dx, dz], rx_send.at[g, dz, dx], rx_recv.at[g, dz, dx])
                value += xbuf[g, dx, dz].astype(jnp.float32)
            if dz:
                comb[g, dz] = value.astype(jnp.bfloat16)
                pending.append(
                    remote(
                        comb.at[g, dz],
                        fin.at[g, dz],
                        rz_send.at[g, dz],
                        rz_recv.at[g, dz],
                        device_at(dz, 0),
                    )
                )
            else:
                fin[g, 0] = value.astype(jnp.bfloat16)

    def finish(g):
        value = fin[g, 0].astype(jnp.float32)
        for dz in range(1, hi):
            arrived(fin.at[g, dz], rz_send.at[g, dz], rz_recv.at[g, dz])
            value += fin[g, dz].astype(jnp.float32)
        out_ref[g] = value.astype(jnp.bfloat16)

    def await_panel(p):
        first = pl.multiple_of((1 - core) * half, LANES)
        if p == 2:
            arrived(wd.at[pl.ds(first, half)], panel_send.at[2, 0], panel_recv.at[2, 0])
            return
        panel_copies[p].wait()
        other_cols = pl.ds(pl.multiple_of(p * full + first, LANES), half)
        for q in range(PARTS):
            part = pl.ds(q * piece, piece)
            arrived(wgu.at[part, other_cols], panel_send.at[p, q], panel_recv.at[p, q])

    def picks_of(slot):
        count = jnp.zeros((1, 1), jnp.float32)
        for g in range(batches):
            marks = tok[g, :, pl.ds(width, LANES)].astype(jnp.float32)
            place = lax.broadcasted_iota(jnp.int32, marks.shape, 1)
            mine = (place >= top) & (place < 2 * top) & (marks == slot.astype(jnp.float32))
            per_lane = jnp.sum(jnp.where(mine, 1.0, 0.0), axis=0, keepdims=True)
            count += jnp.sum(per_lane, axis=1, keepdims=True)
        return count

    send_z(0)
    for p, (src, dst) in enumerate(panels[:2]):
        for q in range(PARTS):
            part = pl.ds(q * piece, piece)
            pending.append(
                remote(
                    src.at[part],
                    dst.at[part],
                    panel_send.at[p, q],
                    panel_recv.at[p, q],
                    sibling,
                )
            )
    panel_copies[2].wait()
    tall = min(ROWS, width)

    @pl.loop(0, width // tall)
    def _(i):
        part = pl.ds(pl.multiple_of(i * tall, tall), tall)
        wd[gate_cols, part] = stage[part, :].T

    turned = wd.at[gate_cols]
    pending.append(remote(turned, turned, panel_send.at[2, 0], panel_recv.at[2, 0], sibling))
    relay_z(0)
    for g in range(1, batches):
        send_z(g)
    await_x(0)
    for g in range(batches):
        if g == 0:
            await_panel(0)
            await_panel(1)
        hidden(g)
        if g == 0:
            await_panel(2)
        result(g)
        if g + 1 < batches:
            relay_z(g + 1)
            await_x(g + 1)
        collect(g)

    tally[0] = jnp.broadcast_to(picks_of(sibling), tally.shape[1:])
    swap = remote(tally.at[0], tally.at[1], tally_sem.at[0], tally_sem.at[1], sibling)
    pending.append(swap)
    count = picks_of(me)
    for g in range(batches):
        finish(g)
    arrived(tally.at[1], tally_sem.at[0], tally_sem.at[1])
    load_ref[...] = (count + tally[1, :1, :1]).astype(jnp.int32)
    for copy in pending:
        copy.wait_send()


def per_device(
    activations,
    pick_weight,
    expert_ids,
    replica,
    old_home,
    new_expert,
    gate_panel,
    up_panel,
    down_panel,
):
    n = lax.axis_size("expert")
    hi, lo = grid_of(n)
    batches, t, width = activations.shape
    half = gate_panel.shape[2]
    total = hi * lo * t
    dma = pltpu.SemaphoreType.DMA
    vmem = pl.BlockSpec(memory_space=pltpu.VMEM)
    hbm = pl.BlockSpec(memory_space=pl.ANY)
    bf16 = jnp.bfloat16
    out, load = pl.pallas_call(
        functools.partial(layer_kernel, hi, lo),
        out_shape=(
            jax.ShapeDtypeStruct(activations.shape, bf16),
            jax.ShapeDtypeStruct((1, 1), jnp.int32),
        ),
        in_specs=[hbm, vmem, vmem, vmem, vmem, vmem, hbm, hbm, hbm],
        out_specs=(vmem, vmem),
        scratch_shapes=[
            pltpu.VMEM((batches, total, width + LANES), bf16),
            pltpu.VMEM((width, 4 * half), bf16),
            pltpu.VMEM((2 * half, width), bf16),
            pltpu.VMEM((width, half), bf16),
            pltpu.VMEM((batches, total, 2 * half), bf16),
            pltpu.VMEM((batches, total, width), bf16),
            pltpu.VMEM((batches, lo, hi, t, width), bf16),
            pltpu.VMEM((batches, hi, t, width), bf16),
            pltpu.VMEM((batches, hi, t, width), bf16),
            pltpu.VMEM((2, 8, LANES), jnp.float32),
            dma((batches + 3,)),
            dma((3, PARTS)),
            dma((3, PARTS)),
            dma((batches, hi)),
            dma((batches, hi)),
            dma((batches, hi, lo)),
            dma((batches, hi, lo)),
            dma((batches, hi, lo)),
            dma((batches, hi, lo)),
            dma((batches, hi)),
            dma((batches, hi)),
            dma((2,)),
        ],
        compiler_params=pltpu.CompilerParams(
            collective_id=0, has_side_effects=True, vmem_limit_bytes=60 * 1024 * 1024
        ),
        cost_estimate=pl.CostEstimate(
            flops=12 * batches * total * width * half,
            bytes_accessed=12 * width * half,
            transcendentals=2 * batches * total * half,
        ),
        name="expert_layer",
    )(
        activations,
        pick_weight.transpose(0, 2, 1),
        expert_ids.transpose(0, 2, 1),
        replica.transpose(0, 2, 1),
        old_home.reshape(1, -1),
        new_expert.reshape(1, -1),
        gate_panel,
        up_panel,
        down_panel,
    )
    return out, load.reshape(1)


def solution(mesh):
    return jax.shard_map(
        per_device,
        mesh=mesh,
        in_specs=(
            P(None, ("groups", "expert"), None),
            P(None, ("groups", "expert"), None),
            P(None, ("groups", "expert"), None),
            P(None, ("groups", "expert"), None),
            P(),
            P("groups"),
            P("expert", None, None),
            P("expert", None, None),
            P("expert", None, None),
        ),
        out_specs=(P(None, ("groups", "expert"), None), P(("groups", "expert"))),
        check_vma=False,
    )
```

```python
import functools
import math

import jax
import jax.numpy as jnp
from jax import lax
from jax.experimental import pallas as pl
from jax.experimental.pallas import tpu as pltpu
from jax.sharding import PartitionSpec as P

MESH = pl.DeviceIdType.MESH
LANES = 128
ROWS = 256
PARTS = 8
DOWN_PARTS = 4


def grid_of(devices):
    chips = devices // 2
    lo = max(d for d in range(1, math.isqrt(chips) + 1) if chips % d == 0)
    return chips // lo, lo


def layer_kernel(
    hi,
    lo,
    act_ref,
    weight_ref,
    ids_ref,
    rep_ref,
    home_ref,
    row_ref,
    gate_ref,
    up_ref,
    down_ref,
    out_ref,
    load_ref,
    tok,
    wgu,
    wd,
    stage,
    hid,
    res,
    xbuf,
    comb,
    fin,
    tally,
    local_sem,
    panel_send,
    panel_recv,
    z_send,
    z_recv,
    x_send,
    x_recv,
    rx_send,
    rx_recv,
    rz_send,
    rz_recv,
    tally_sem,
):
    batches, t, width = act_ref.shape
    top = ids_ref.shape[1]
    half = gate_ref.shape[2]
    full = 2 * half
    piece = width // PARTS
    strip = half // DOWN_PARTS
    me = lax.axis_index("expert")
    core = lax.rem(me, 2)
    chip = me // 2
    xi = lax.rem(chip, lo)
    zi = chip // lo
    sibling = chip * 2 + (1 - core)

    def chip_at(dz, dx):
        z = lax.rem(zi + dz + hi, hi)
        x = lax.rem(xi + dx + lo, lo)
        return z * lo + x

    def device_at(dz, dx):
        return chip_at(dz, dx) * 2 + core

    def rows(place):
        return pl.ds(pl.multiple_of(place * t, t), t)

    groups = lax.axis_size("groups")
    group = lax.axis_index("groups")

    def remote(src, dst, send, recv, device, turn=0):
        copy = pltpu.make_async_remote_copy(
            src_ref=src,
            dst_ref=dst,
            send_sem=send,
            recv_sem=recv,
            device_id={"groups": lax.rem(group + turn, groups), "expert": device},
            device_id_type=MESH,
        )
        copy.start()
        return copy

    def arrived(ref, send, recv):
        pltpu.make_async_remote_copy(
            src_ref=ref,
            dst_ref=ref,
            send_sem=send,
            recv_sem=recv,
            device_id={"expert": sibling},
            device_id_type=MESH,
        ).wait_recv()

    def local(src, dst, sem):
        copy = pltpu.make_async_copy(src, dst, sem)
        copy.start()
        return copy

    peers = [device_at(dz, 0) for dz in range(1, hi)]
    peers += [device_at(0, dx) for dx in range(1, lo)] + [sibling]
    barrier = pltpu.get_barrier_semaphore()
    for peer in peers:
        pl.semaphore_signal(barrier, inc=1, device_id={"expert": peer}, device_id_type=MESH)

    turns = sorted({1 % groups, (groups - 1) % groups} - {0})
    for turn in turns:
        other = {"groups": lax.rem(group + turn, groups), "expert": sibling}
        pl.semaphore_signal(barrier, inc=1, device_id=other, device_id_type=MESH)

    gate_cols = pl.ds(pl.multiple_of(core * half, LANES), half)
    up_cols = pl.ds(pl.multiple_of(full + core * half, LANES), half)
    panels = (
        (gate_ref.at[0], wgu.at[:, gate_cols]),
        (up_ref.at[0], wgu.at[:, up_cols]),
        (down_ref.at[0], stage),
    )
    act_copies = [
        local(act_ref.at[g], tok.at[g, rows(chip), pl.ds(0, width)], local_sem.at[g])
        for g in range(batches)
    ]
    panel_copies = [
        local(src, dst, local_sem.at[batches + p]) for p, (src, dst) in enumerate(panels)
    ]

    def upright(line):
        count = line.shape[1]
        shape = (count, count)
        same = lax.broadcasted_iota(jnp.int32, shape, 0) == lax.broadcasted_iota(
            jnp.int32, shape, 1
        )
        return jnp.sum(jnp.where(same, line, jnp.zeros_like(line)), axis=1, keepdims=True)

    row = row_ref[...]
    slots = row.shape[1]
    s_lane = lax.broadcasted_iota(jnp.int32, (slots, slots), 1)
    s_row = lax.broadcasted_iota(jnp.int32, (slots, slots), 0)
    earlier = (upright(row) == row) & (s_row < s_lane)
    ranks = jnp.sum(earlier.astype(jnp.int32), axis=0, keepdims=True)
    homes = home_ref[...]
    lane_slot = lax.broadcasted_iota(jnp.int32, (t, slots), 1)
    lane_expert = lax.broadcasted_iota(jnp.int32, (t, homes.shape[1]), 1)
    lane = lax.broadcasted_iota(jnp.int32, (t, LANES), 1)
    for g in range(batches):
        marks = jnp.zeros((t, LANES), jnp.float32)
        for k in range(top):
            ids = upright(ids_ref[g, k : k + 1, :])
            rep = upright(rep_ref[g, k : k + 1, :])
            weight = upright(weight_ref[g, k : k + 1, :])
            home = jnp.sum(jnp.where(lane_expert == ids, homes, 0), axis=1, keepdims=True)
            match = (row == ids) & (ranks == rep)
            slot = jnp.sum(jnp.where(match, lane_slot, 0), axis=1, keepdims=True)
            first = weight.astype(jnp.bfloat16).astype(jnp.float32)
            second = (weight - first).astype(jnp.bfloat16).astype(jnp.float32)
            third = weight - first - second
            parts = (home.astype(jnp.float32), slot.astype(jnp.float32), first, second, third)
            for place, part in enumerate(parts):
                marks = jnp.where(lane == place * top + k, part, marks)
        tok[g, rows(chip), pl.ds(width, LANES)] = marks.astype(jnp.bfloat16)

    pl.semaphore_wait(barrier, len(peers) + len(turns))

    pending = []

    def across(g, dz):
        block = tok.at[g, rows(chip_at(-dz, 0))]
        for dx in range(1, lo):
            pending.append(
                remote(
                    block, block, x_send.at[g, dz, dx], x_recv.at[g, dz, dx], device_at(0, dx)
                )
            )

    def send_z(g):
        act_copies[g].wait()
        block = tok.at[g, rows(chip)]
        for dz in range(1, hi):
            pending.append(
                remote(block, block, z_send.at[g, dz], z_recv.at[g, dz], device_at(dz, 0))
            )
        across(g, 0)

    def relay_z(g):
        for dz in range(1, hi):
            arrived(tok.at[g, rows(chip_at(-dz, 0))], z_send.at[g, dz], z_recv.at[g, dz])
            across(g, dz)

    def await_x(g):
        for dz in range(hi):
            for dx in range(1, lo):
                arrived(
                    tok.at[g, rows(chip_at(-dz, -dx))],
                    x_send.at[g, dz, dx],
                    x_recv.at[g, dz, dx],
                )

    total = hi * lo * t
    step = min(ROWS, total)

    def chunks(body):
        if total == step:
            body(pl.ds(0, step))
        else:

            @pl.loop(0, total // step)
            def _(i):
                body(pl.ds(pl.multiple_of(i * step, step), step))

    def hidden(g):
        def body(part):
            both = jnp.dot(
                tok[g, part, pl.ds(0, width)], wgu[...], preferred_element_type=jnp.float32
            )
            gate, up = both[:, :full], both[:, full:]
            hid[g, part, :] = (gate / (1.0 + jnp.exp(-gate)) * up).astype(jnp.bfloat16)

        chunks(body)

    def result(g):
        def body(part):
            value = jnp.dot(hid[g, part, :], wd[...], preferred_element_type=jnp.float32)
            value = value.astype(jnp.bfloat16).astype(jnp.float32)
            marks = tok[g, part, pl.ds(width, LANES)].astype(jnp.float32)
            scale = jnp.zeros((step, 1), jnp.float32)
            for k in range(top):
                home, _, first, second, third = (
                    marks[:, p * top + k : p * top + k + 1] for p in range(5)
                )
                weight = first + (second + third)
                scale += jnp.where(home == chip.astype(jnp.float32), weight, 0.0)
            res[g, part, :] = (value * scale).astype(jnp.bfloat16)

        chunks(body)
        for dz in back_order:
            for dx in range(1, lo):
                pending.append(
                    remote(
                        res.at[g, rows(chip_at(dz, dx))],
                        xbuf.at[g, dx, dz],
                        rx_send.at[g, dz, dx],
                        rx_recv.at[g, dz, dx],
                        device_at(0, dx),
                    )
                )

    back_order = list(range(1, hi)) + [0]

    def collect(g):
        for dz in back_order:
            value = res[g, rows(chip_at(dz, 0)), :].astype(jnp.float32)
            for dx in range(1, lo):
                arrived(xbuf.at[g, dx, dz], rx_send.at[g, dz, dx], rx_recv.at[g, dz, dx])
                value += xbuf[g, dx, dz].astype(jnp.float32)
            if dz:
                comb[g, dz] = value.astype(jnp.bfloat16)
                pending.append(
                    remote(
                        comb.at[g, dz],
                        fin.at[g, dz],
                        rz_send.at[g, dz],
                        rz_recv.at[g, dz],
                        device_at(dz, 0),
                    )
                )
            else:
                fin[g, 0] = value.astype(jnp.bfloat16)

    def finish(g):
        value = fin[g, 0].astype(jnp.float32)
        for dz in range(1, hi):
            arrived(fin.at[g, dz], rz_send.at[g, dz], rz_recv.at[g, dz])
            value += fin[g, dz].astype(jnp.float32)
        out_ref[g] = value.astype(jnp.bfloat16)

    def await_panel(p):
        first = pl.multiple_of((1 - core) * half, LANES)
        if p == 2:
            for q in range(DOWN_PARTS):
                part = pl.ds(pl.multiple_of((1 - core) * half + q * strip, 16), strip)
                arrived(wd.at[part], panel_send.at[2, q], panel_recv.at[2, q])
            return
        panel_copies[p].wait()
        other_cols = pl.ds(pl.multiple_of(p * full + first, LANES), half)
        for q in range(PARTS):
            part = pl.ds(q * piece, piece)
            arrived(wgu.at[part, other_cols], panel_send.at[p, q], panel_recv.at[p, q])

    def picks_of(slot):
        count = jnp.zeros((1, 1), jnp.float32)
        for g in range(batches):
            marks = tok[g, :, pl.ds(width, LANES)].astype(jnp.float32)
            place = lax.broadcasted_iota(jnp.int32, marks.shape, 1)
            mine = (place >= top) & (place < 2 * top) & (marks == slot.astype(jnp.float32))
            per_lane = jnp.sum(jnp.where(mine, 1.0, 0.0), axis=0, keepdims=True)
            count += jnp.sum(per_lane, axis=1, keepdims=True)
        return count

    send_z(0)
    for p, (src, dst) in enumerate(panels[:2]):
        for q in range(PARTS):
            part = pl.ds(q * piece, piece)
            pending.append(
                remote(
                    src.at[part],
                    dst.at[part],
                    panel_send.at[p, q],
                    panel_recv.at[p, q],
                    sibling,
                    turn=int(q == 0),
                )
            )
    panel_copies[2].wait()
    tall = min(ROWS, width)

    @pl.loop(0, width // tall)
    def _(i):
        part = pl.ds(pl.multiple_of(i * tall, tall), tall)
        wd[gate_cols, part] = stage[part, :].T

    for q in range(DOWN_PARTS):
        turned = wd.at[pl.ds(pl.multiple_of(core * half + q * strip, 16), strip)]
        pending.append(
            remote(
                turned,
                turned,
                panel_send.at[2, q],
                panel_recv.at[2, q],
                sibling,
                turn=int(q == 0),
            )
        )
    relay_z(0)
    for g in range(1, batches):
        send_z(g)
    await_x(0)
    for g in range(batches):
        if g == 0:
            await_panel(0)
            await_panel(1)
        hidden(g)
        if g == 0:
            await_panel(2)
        result(g)
        if g + 1 < batches:
            relay_z(g + 1)
            await_x(g + 1)
        collect(g)

    tally[0] = jnp.broadcast_to(picks_of(sibling), tally.shape[1:])
    swap = remote(tally.at[0], tally.at[1], tally_sem.at[0], tally_sem.at[1], sibling)
    pending.append(swap)
    count = picks_of(me)
    for g in range(batches):
        finish(g)
    arrived(tally.at[1], tally_sem.at[0], tally_sem.at[1])
    load_ref[...] = (count + tally[1, :1, :1]).astype(jnp.int32)
    for copy in pending:
        copy.wait_send()


def per_device(
    activations,
    pick_weight,
    expert_ids,
    replica,
    old_home,
    new_expert,
    gate_panel,
    up_panel,
    down_panel,
):
    n = lax.axis_size("expert")
    hi, lo = grid_of(n)
    batches, t, width = activations.shape
    half = gate_panel.shape[2]
    total = hi * lo * t
    dma = pltpu.SemaphoreType.DMA
    vmem = pl.BlockSpec(memory_space=pltpu.VMEM)
    hbm = pl.BlockSpec(memory_space=pl.ANY)
    bf16 = jnp.bfloat16
    out, load = pl.pallas_call(
        functools.partial(layer_kernel, hi, lo),
        out_shape=(
            jax.ShapeDtypeStruct(activations.shape, bf16),
            jax.ShapeDtypeStruct((1, 1), jnp.int32),
        ),
        in_specs=[hbm, vmem, vmem, vmem, vmem, vmem, hbm, hbm, hbm],
        out_specs=(vmem, vmem),
        scratch_shapes=[
            pltpu.VMEM((batches, total, width + LANES), bf16),
            pltpu.VMEM((width, 4 * half), bf16),
            pltpu.VMEM((2 * half, width), bf16),
            pltpu.VMEM((width, half), bf16),
            pltpu.VMEM((batches, total, 2 * half), bf16),
            pltpu.VMEM((batches, total, width), bf16),
            pltpu.VMEM((batches, lo, hi, t, width), bf16),
            pltpu.VMEM((batches, hi, t, width), bf16),
            pltpu.VMEM((batches, hi, t, width), bf16),
            pltpu.VMEM((2, 8, LANES), jnp.float32),
            dma((batches + 3,)),
            dma((3, PARTS)),
            dma((3, PARTS)),
            dma((batches, hi)),
            dma((batches, hi)),
            dma((batches, hi, lo)),
            dma((batches, hi, lo)),
            dma((batches, hi, lo)),
            dma((batches, hi, lo)),
            dma((batches, hi)),
            dma((batches, hi)),
            dma((2,)),
        ],
        compiler_params=pltpu.CompilerParams(
            collective_id=0, has_side_effects=True, vmem_limit_bytes=60 * 1024 * 1024
        ),
        cost_estimate=pl.CostEstimate(
            flops=12 * batches * total * width * half,
            bytes_accessed=12 * width * half,
            transcendentals=2 * batches * total * half,
        ),
        name="expert_layer",
    )(
        activations,
        pick_weight.transpose(0, 2, 1),
        expert_ids.transpose(0, 2, 1),
        replica.transpose(0, 2, 1),
        old_home.reshape(1, -1),
        new_expert.reshape(1, -1),
        gate_panel,
        up_panel,
        down_panel,
    )
    return out, load.reshape(1)


def solution(mesh):
    return jax.shard_map(
        per_device,
        mesh=mesh,
        in_specs=(
            P(None, ("groups", "expert"), None),
            P(None, ("groups", "expert"), None),
            P(None, ("groups", "expert"), None),
            P(None, ("groups", "expert"), None),
            P(),
            P("groups"),
            P("expert", None, None),
            P("expert", None, None),
            P("expert", None, None),
        ),
        out_specs=(P(None, ("groups", "expert"), None), P(("groups", "expert"))),
        check_vma=False,
    )
```

```python
import functools
import math

import jax
import jax.numpy as jnp
from jax import lax
from jax.experimental import pallas as pl
from jax.experimental.pallas import tpu as pltpu
from jax.sharding import PartitionSpec as P

MESH = pl.DeviceIdType.MESH
LANES = 128
ROWS = 256
PARTS = 4


def grid_of(devices):
    chips = devices // 2
    lo = max(d for d in range(1, math.isqrt(chips) + 1) if chips % d == 0)
    return chips // lo, lo


def layer_kernel(
    hi,
    lo,
    act_ref,
    weight_ref,
    ids_ref,
    rep_ref,
    home_ref,
    row_ref,
    gate_ref,
    up_ref,
    down_ref,
    out_ref,
    load_ref,
    tok,
    wgu,
    wd,
    stage,
    hid,
    res,
    xbuf,
    comb,
    tally,
    local_sem,
    panel_send,
    panel_recv,
    z_send,
    z_recv,
    x_send,
    x_recv,
    rx_send,
    rx_recv,
    rz_send,
    rz_recv,
    tally_sem,
):
    batches, t, width = act_ref.shape
    top = ids_ref.shape[1]
    half = gate_ref.shape[2]
    full = 2 * half
    piece = width // PARTS
    me = lax.axis_index("expert")
    core = lax.rem(me, 2)
    chip = me // 2
    xi = lax.rem(chip, lo)
    zi = chip // lo
    sibling = chip * 2 + (1 - core)

    def chip_at(dz, dx):
        z = lax.rem(zi + dz + hi, hi)
        x = lax.rem(xi + dx + lo, lo)
        return z * lo + x

    def device_at(dz, dx):
        return chip_at(dz, dx) * 2 + core

    def rows(place):
        return pl.ds(pl.multiple_of(place * t, t), t)

    def remote(src, dst, send, recv, device):
        copy = pltpu.make_async_remote_copy(
            src_ref=src,
            dst_ref=dst,
            send_sem=send,
            recv_sem=recv,
            device_id={"expert": device},
            device_id_type=MESH,
        )
        copy.start()
        return copy

    def arrived(ref, send, recv):
        pltpu.make_async_remote_copy(
            src_ref=ref,
            dst_ref=ref,
            send_sem=send,
            recv_sem=recv,
            device_id={"expert": sibling},
            device_id_type=MESH,
        ).wait_recv()

    def local(src, dst, sem):
        copy = pltpu.make_async_copy(src, dst, sem)
        copy.start()
        return copy

    peers = [device_at(dz, 0) for dz in range(1, hi)]
    peers += [device_at(0, dx) for dx in range(1, lo)] + [sibling]
    barrier = pltpu.get_barrier_semaphore()
    for peer in peers:
        pl.semaphore_signal(barrier, inc=1, device_id={"expert": peer}, device_id_type=MESH)

    gate_cols = pl.ds(pl.multiple_of(core * half, LANES), half)
    up_cols = pl.ds(pl.multiple_of(full + core * half, LANES), half)
    panels = (
        (gate_ref.at[0], wgu.at[:, gate_cols]),
        (up_ref.at[0], wgu.at[:, up_cols]),
        (down_ref.at[0], stage),
    )
    act_copies = [
        local(act_ref.at[g], tok.at[g, rows(chip), pl.ds(0, width)], local_sem.at[g])
        for g in range(batches)
    ]
    panel_copies = [
        local(src, dst, local_sem.at[batches + p]) for p, (src, dst) in enumerate(panels)
    ]

    def upright(line):
        count = line.shape[1]
        shape = (count, count)
        same = lax.broadcasted_iota(jnp.int32, shape, 0) == lax.broadcasted_iota(
            jnp.int32, shape, 1
        )
        return jnp.sum(jnp.where(same, line, jnp.zeros_like(line)), axis=1, keepdims=True)

    row = row_ref[...]
    slots = row.shape[1]
    s_lane = lax.broadcasted_iota(jnp.int32, (slots, slots), 1)
    s_row = lax.broadcasted_iota(jnp.int32, (slots, slots), 0)
    earlier = (upright(row) == row) & (s_row < s_lane)
    ranks = jnp.sum(earlier.astype(jnp.int32), axis=0, keepdims=True)
    homes = home_ref[...]
    lane_slot = lax.broadcasted_iota(jnp.int32, (t, slots), 1)
    lane_expert = lax.broadcasted_iota(jnp.int32, (t, homes.shape[1]), 1)
    lane = lax.broadcasted_iota(jnp.int32, (t, LANES), 1)
    for g in range(batches):
        marks = jnp.zeros((t, LANES), jnp.float32)
        for k in range(top):
            ids = upright(ids_ref[g, k : k + 1, :])
            rep = upright(rep_ref[g, k : k + 1, :])
            weight = upright(weight_ref[g, k : k + 1, :])
            home = jnp.sum(jnp.where(lane_expert == ids, homes, 0), axis=1, keepdims=True)
            match = (row == ids) & (ranks == rep)
            slot = jnp.sum(jnp.where(match, lane_slot, 0), axis=1, keepdims=True)
            first = weight.astype(jnp.bfloat16).astype(jnp.float32)
            second = (weight - first).astype(jnp.bfloat16).astype(jnp.float32)
            third = weight - first - second
            parts = (home.astype(jnp.float32), slot.astype(jnp.float32), first, second, third)
            for place, part in enumerate(parts):
                marks = jnp.where(lane == place * top + k, part, marks)
        tok[g, rows(chip), pl.ds(width, LANES)] = marks.astype(jnp.bfloat16)

    pl.semaphore_wait(barrier, len(peers))

    pending = []

    def across(g, dz):
        block = tok.at[g, rows(chip_at(-dz, 0))]
        for dx in range(1, lo):
            pending.append(
                remote(
                    block, block, x_send.at[g, dz, dx], x_recv.at[g, dz, dx], device_at(0, dx)
                )
            )

    def send_z(g):
        act_copies[g].wait()
        block = tok.at[g, rows(chip)]
        for dz in range(1, hi):
            pending.append(
                remote(block, block, z_send.at[g, dz], z_recv.at[g, dz], device_at(dz, 0))
            )
        across(g, 0)

    def relay_z(g):
        for dz in range(1, hi):
            arrived(tok.at[g, rows(chip_at(-dz, 0))], z_send.at[g, dz], z_recv.at[g, dz])
            across(g, dz)

    def await_x(g):
        for dz in range(hi):
            for dx in range(1, lo):
                arrived(
                    tok.at[g, rows(chip_at(-dz, -dx))],
                    x_send.at[g, dz, dx],
                    x_recv.at[g, dz, dx],
                )

    total = hi * lo * t
    step = min(ROWS, total)

    def chunks(body):
        if total == step:
            body(pl.ds(0, step))
        else:

            @pl.loop(0, total // step)
            def _(i):
                body(pl.ds(pl.multiple_of(i * step, step), step))

    def hidden(g):
        def body(part):
            both = jnp.dot(
                tok[g, part, pl.ds(0, width)], wgu[...], preferred_element_type=jnp.float32
            )
            gate, up = both[:, :full], both[:, full:]
            hid[g, part, :] = (gate / (1.0 + jnp.exp(-gate)) * up).astype(jnp.bfloat16)

        chunks(body)

    def result(g):
        def body(part):
            value = jnp.dot(hid[g, part, :], wd[...], preferred_element_type=jnp.float32)
            value = value.astype(jnp.bfloat16).astype(jnp.float32)
            marks = tok[g, part, pl.ds(width, LANES)].astype(jnp.float32)
            scale = jnp.zeros((step, 1), jnp.float32)
            for k in range(top):
                home, _, first, second, third = (
                    marks[:, p * top + k : p * top + k + 1] for p in range(5)
                )
                weight = first + (second + third)
                scale += jnp.where(home == chip.astype(jnp.float32), weight, 0.0)
            res[g, part, :] = (value * scale).astype(jnp.bfloat16)

        chunks(body)
        for dz in back_order:
            for dx in range(1, lo):
                pending.append(
                    remote(
                        res.at[g, rows(chip_at(dz, dx))],
                        xbuf.at[g, dx, dz],
                        rx_send.at[g, dz, dx],
                        rx_recv.at[g, dz, dx],
                        device_at(0, dx),
                    )
                )

    back_order = list(range(1, hi)) + [0]

    def collect(g):
        for dz in back_order:
            value = res[g, rows(chip_at(dz, 0)), :].astype(jnp.float32)
            for dx in range(1, lo):
                arrived(xbuf.at[g, dx, dz], rx_send.at[g, dz, dx], rx_recv.at[g, dz, dx])
                value += xbuf[g, dx, dz].astype(jnp.float32)
            comb[g, dz] = value.astype(jnp.bfloat16)
            if dz:
                pending.append(
                    remote(
                        comb.at[g, dz],
                        out_ref.at[dz, g],
                        rz_send.at[g, dz],
                        rz_recv.at[g, dz],
                        device_at(dz, 0),
                    )
                )
            else:
                own_copies.append(local(comb.at[g, 0], out_ref.at[0, g], rz_send.at[g, 0]))

    own_copies = []

    def finish(g):
        own_copies[g].wait()
        for dz in range(1, hi):
            arrived(out_ref.at[dz, g], rz_send.at[g, dz], rz_recv.at[g, dz])

    def await_panel(p):
        first = pl.multiple_of((1 - core) * half, LANES)
        if p == 2:
            arrived(wd.at[pl.ds(first, half)], panel_send.at[2, 0], panel_recv.at[2, 0])
            return
        panel_copies[p].wait()
        other_cols = pl.ds(pl.multiple_of(p * full + first, LANES), half)
        for q in range(PARTS):
            part = pl.ds(q * piece, piece)
            arrived(wgu.at[part, other_cols], panel_send.at[p, q], panel_recv.at[p, q])

    def picks_of(slot):
        count = jnp.zeros((1, 1), jnp.float32)
        for g in range(batches):
            marks = tok[g, :, pl.ds(width, LANES)].astype(jnp.float32)
            place = lax.broadcasted_iota(jnp.int32, marks.shape, 1)
            mine = (place >= top) & (place < 2 * top) & (marks == slot.astype(jnp.float32))
            per_lane = jnp.sum(jnp.where(mine, 1.0, 0.0), axis=0, keepdims=True)
            count += jnp.sum(per_lane, axis=1, keepdims=True)
        return count

    send_z(0)
    for p, (src, dst) in enumerate(panels[:2]):
        for q in range(PARTS):
            part = pl.ds(q * piece, piece)
            pending.append(
                remote(
                    src.at[part],
                    dst.at[part],
                    panel_send.at[p, q],
                    panel_recv.at[p, q],
                    sibling,
                )
            )
    panel_copies[2].wait()
    tall = min(ROWS, width)

    @pl.loop(0, width // tall)
    def _(i):
        part = pl.ds(pl.multiple_of(i * tall, tall), tall)
        wd[gate_cols, part] = stage[part, :].T

    turned = wd.at[gate_cols]
    pending.append(remote(turned, turned, panel_send.at[2, 0], panel_recv.at[2, 0], sibling))
    relay_z(0)
    for g in range(1, batches):
        send_z(g)
    await_x(0)
    for g in range(batches):
        if g == 0:
            await_panel(0)
            await_panel(1)
        hidden(g)
        if g == 0:
            await_panel(2)
        result(g)
        if g + 1 < batches:
            relay_z(g + 1)
            await_x(g + 1)
        collect(g)

    tally[0] = jnp.broadcast_to(picks_of(sibling), tally.shape[1:])
    swap = remote(tally.at[0], tally.at[1], tally_sem.at[0], tally_sem.at[1], sibling)
    pending.append(swap)
    count = picks_of(me)
    for g in range(batches):
        finish(g)
    arrived(tally.at[1], tally_sem.at[0], tally_sem.at[1])
    load_ref[...] = (count + tally[1, :1, :1]).astype(jnp.int32)
    for copy in pending:
        copy.wait_send()


def per_device(
    activations,
    pick_weight,
    expert_ids,
    replica,
    old_home,
    new_expert,
    gate_panel,
    up_panel,
    down_panel,
):
    n = lax.axis_size("expert")
    hi, lo = grid_of(n)
    batches, t, width = activations.shape
    half = gate_panel.shape[2]
    total = hi * lo * t
    dma = pltpu.SemaphoreType.DMA
    vmem = pl.BlockSpec(memory_space=pltpu.VMEM)
    hbm = pl.BlockSpec(memory_space=pl.ANY)
    bf16 = jnp.bfloat16
    parts, load = pl.pallas_call(
        functools.partial(layer_kernel, hi, lo),
        out_shape=(
            jax.ShapeDtypeStruct((hi,) + activations.shape, bf16),
            jax.ShapeDtypeStruct((1, 1), jnp.int32),
        ),
        in_specs=[hbm, vmem, vmem, vmem, vmem, vmem, hbm, hbm, hbm],
        out_specs=(hbm, vmem),
        scratch_shapes=[
            pltpu.VMEM((batches, total, width + LANES), bf16),
            pltpu.VMEM((width, 4 * half), bf16),
            pltpu.VMEM((2 * half, width), bf16),
            pltpu.VMEM((width, half), bf16),
            pltpu.VMEM((batches, total, 2 * half), bf16),
            pltpu.VMEM((batches, total, width), bf16),
            pltpu.VMEM((batches, lo, hi, t, width), bf16),
            pltpu.VMEM((batches, hi, t, width), bf16),
            pltpu.VMEM((2, 8, LANES), jnp.float32),
            dma((batches + 3,)),
            dma((3, PARTS)),
            dma((3, PARTS)),
            dma((batches, hi)),
            dma((batches, hi)),
            dma((batches, hi, lo)),
            dma((batches, hi, lo)),
            dma((batches, hi, lo)),
            dma((batches, hi, lo)),
            dma((batches, hi)),
            dma((batches, hi)),
            dma((2,)),
        ],
        compiler_params=pltpu.CompilerParams(
            collective_id=0, has_side_effects=True, vmem_limit_bytes=60 * 1024 * 1024
        ),
        cost_estimate=pl.CostEstimate(
            flops=12 * batches * total * width * half,
            bytes_accessed=12 * width * half,
            transcendentals=2 * batches * total * half,
        ),
        name="expert_layer",
    )(
        activations,
        pick_weight.transpose(0, 2, 1),
        expert_ids.transpose(0, 2, 1),
        replica.transpose(0, 2, 1),
        old_home.reshape(1, -1),
        new_expert.reshape(1, -1),
        gate_panel,
        up_panel,
        down_panel,
    )
    out = jnp.sum(parts.astype(jnp.float32), axis=0).astype(bf16)
    return out, load.reshape(1)


def solution(mesh):
    return jax.shard_map(
        per_device,
        mesh=mesh,
        in_specs=(
            P(None, ("groups", "expert"), None),
            P(None, ("groups", "expert"), None),
            P(None, ("groups", "expert"), None),
            P(None, ("groups", "expert"), None),
            P(),
            P("groups"),
            P("expert", None, None),
            P("expert", None, None),
            P("expert", None, None),
        ),
        out_specs=(P(None, ("groups", "expert"), None), P(("groups", "expert"))),
        check_vma=False,
    )
```

```python
import functools
import math

import jax
import jax.numpy as jnp
from jax import lax
from jax.experimental import pallas as pl
from jax.experimental.pallas import tpu as pltpu
from jax.sharding import PartitionSpec as P

MESH = pl.DeviceIdType.MESH
LANES = 128
ROWS = 256
PARTS = 4


def grid_of(devices):
    chips = devices // 2
    lo = max(d for d in range(1, math.isqrt(chips) + 1) if chips % d == 0)
    return chips // lo, lo


def layer_kernel(
    hi,
    lo,
    act_ref,
    weight_ref,
    ids_ref,
    rep_ref,
    home_ref,
    row_ref,
    gate_ref,
    up_ref,
    down_ref,
    out_ref,
    load_ref,
    tok,
    wgu,
    wd,
    stage,
    hid,
    res,
    xbuf,
    comb,
    fin,
    tally,
    local_sem,
    panel_send,
    panel_recv,
    z_send,
    z_recv,
    x_send,
    x_recv,
    rx_send,
    rx_recv,
    rz_send,
    rz_recv,
    tally_sem,
):
    batches, t, width = act_ref.shape
    top = ids_ref.shape[1]
    half = gate_ref.shape[2]
    full = 2 * half
    piece = width // PARTS
    me = lax.axis_index("expert")
    core = lax.rem(me, 2)
    chip = me // 2
    xi = lax.rem(chip, lo)
    zi = chip // lo
    sibling = chip * 2 + (1 - core)

    def chip_at(dz, dx):
        z = lax.rem(zi + dz + hi, hi)
        x = lax.rem(xi + dx + lo, lo)
        return z * lo + x

    def device_at(dz, dx):
        return chip_at(dz, dx) * 2 + core

    def rows(place):
        return pl.ds(pl.multiple_of(place * t, t), t)

    def remote(src, dst, send, recv, device):
        copy = pltpu.make_async_remote_copy(
            src_ref=src,
            dst_ref=dst,
            send_sem=send,
            recv_sem=recv,
            device_id={"expert": device},
            device_id_type=MESH,
        )
        copy.start()
        return copy

    def arrived(ref, send, recv):
        pltpu.make_async_remote_copy(
            src_ref=ref,
            dst_ref=ref,
            send_sem=send,
            recv_sem=recv,
            device_id={"expert": sibling},
            device_id_type=MESH,
        ).wait_recv()

    def local(src, dst, sem):
        copy = pltpu.make_async_copy(src, dst, sem)
        copy.start()
        return copy

    peers = [device_at(dz, 0) for dz in range(1, hi)]
    peers += [device_at(0, dx) for dx in range(1, lo)] + [sibling]
    barrier = pltpu.get_barrier_semaphore()
    for peer in peers:
        pl.semaphore_signal(barrier, inc=1, device_id={"expert": peer}, device_id_type=MESH)

    gate_cols = pl.ds(pl.multiple_of(core * half, LANES), half)
    up_cols = pl.ds(pl.multiple_of(full + core * half, LANES), half)
    panels = (
        (gate_ref.at[0], wgu.at[:, gate_cols]),
        (up_ref.at[0], wgu.at[:, up_cols]),
        (down_ref.at[0], stage),
    )
    act_copies = [
        local(act_ref.at[g], tok.at[g, rows(chip), pl.ds(0, width)], local_sem.at[g])
        for g in range(batches)
    ]
    panel_copies = [
        local(src, dst, local_sem.at[batches + p]) for p, (src, dst) in enumerate(panels)
    ]

    def upright(line):
        count = line.shape[1]
        shape = (count, count)
        same = lax.broadcasted_iota(jnp.int32, shape, 0) == lax.broadcasted_iota(
            jnp.int32, shape, 1
        )
        return jnp.sum(jnp.where(same, line, jnp.zeros_like(line)), axis=1, keepdims=True)

    row = row_ref[...]
    slots = row.shape[1]
    s_lane = lax.broadcasted_iota(jnp.int32, (slots, slots), 1)
    s_row = lax.broadcasted_iota(jnp.int32, (slots, slots), 0)
    earlier = (upright(row) == row) & (s_row < s_lane)
    ranks = jnp.sum(earlier.astype(jnp.int32), axis=0, keepdims=True)
    homes = home_ref[...]
    lane_slot = lax.broadcasted_iota(jnp.int32, (t, slots), 1)
    lane_expert = lax.broadcasted_iota(jnp.int32, (t, homes.shape[1]), 1)
    lane = lax.broadcasted_iota(jnp.int32, (t, LANES), 1)
    for g in range(batches):
        marks = jnp.zeros((t, LANES), jnp.float32)
        for k in range(top):
            ids = upright(ids_ref[g, k : k + 1, :])
            rep = upright(rep_ref[g, k : k + 1, :])
            weight = upright(weight_ref[g, k : k + 1, :])
            home = jnp.sum(jnp.where(lane_expert == ids, homes, 0), axis=1, keepdims=True)
            match = (row == ids) & (ranks == rep)
            slot = jnp.sum(jnp.where(match, lane_slot, 0), axis=1, keepdims=True)
            first = weight.astype(jnp.bfloat16).astype(jnp.float32)
            second = (weight - first).astype(jnp.bfloat16).astype(jnp.float32)
            third = weight - first - second
            parts = (home.astype(jnp.float32), slot.astype(jnp.float32), first, second, third)
            for place, part in enumerate(parts):
                marks = jnp.where(lane == place * top + k, part, marks)
        tok[g, rows(chip), pl.ds(width, LANES)] = marks.astype(jnp.bfloat16)

    pl.semaphore_wait(barrier, len(peers))

    pending = []

    def across(g, dz):
        block = tok.at[g, rows(chip_at(-dz, 0))]
        for dx in range(1, lo):
            pending.append(
                remote(
                    block, block, x_send.at[g, dz, dx], x_recv.at[g, dz, dx], device_at(0, dx)
                )
            )

    def send_z(g):
        act_copies[g].wait()
        block = tok.at[g, rows(chip)]
        for dz in range(1, hi):
            pending.append(
                remote(block, block, z_send.at[g, dz], z_recv.at[g, dz], device_at(dz, 0))
            )
        across(g, 0)

    def relay_z(g):
        for dz in range(1, hi):
            arrived(tok.at[g, rows(chip_at(-dz, 0))], z_send.at[g, dz], z_recv.at[g, dz])
            across(g, dz)

    def await_x(g):
        for dz in range(hi):
            for dx in range(1, lo):
                arrived(
                    tok.at[g, rows(chip_at(-dz, -dx))],
                    x_send.at[g, dz, dx],
                    x_recv.at[g, dz, dx],
                )

    total = hi * lo * t
    step = min(ROWS, total)

    def chunks(body):
        if total == step:
            body(pl.ds(0, step))
        else:

            @pl.loop(0, total // step)
            def _(i):
                body(pl.ds(pl.multiple_of(i * step, step), step))

    def hidden(g):
        def body(part):
            both = jnp.dot(
                tok[g, part, pl.ds(0, width)], wgu[...], preferred_element_type=jnp.float32
            )
            gate, up = both[:, :full], both[:, full:]
            hid[g, part, :] = (gate / (1.0 + jnp.exp(-gate)) * up).astype(jnp.bfloat16)

        chunks(body)

    def result(g):
        def body(part):
            value = jnp.dot(hid[g, part, :], wd[...], preferred_element_type=jnp.float32)
            value = value.astype(jnp.bfloat16).astype(jnp.float32)
            marks = tok[g, part, pl.ds(width, LANES)].astype(jnp.float32)
            scale = jnp.zeros((step, 1), jnp.float32)
            for k in range(top):
                home, _, first, second, third = (
                    marks[:, p * top + k : p * top + k + 1] for p in range(5)
                )
                weight = first + (second + third)
                scale += jnp.where(home == chip.astype(jnp.float32), weight, 0.0)
            res[g, part, :] = (value * scale).astype(jnp.bfloat16)

        chunks(body)
        for dz in back_order:
            for dx in range(1, lo):
                pending.append(
                    remote(
                        res.at[g, rows(chip_at(dz, dx))],
                        xbuf.at[g, dx, dz],
                        rx_send.at[g, dz, dx],
                        rx_recv.at[g, dz, dx],
                        device_at(0, dx),
                    )
                )

    back_order = list(range(1, hi)) + [0]

    def collect(g):
        for dz in back_order:
            value = res[g, rows(chip_at(dz, 0)), :].astype(jnp.float32)
            for dx in range(1, lo):
                arrived(xbuf.at[g, dx, dz], rx_send.at[g, dz, dx], rx_recv.at[g, dz, dx])
                value += xbuf[g, dx, dz].astype(jnp.float32)
            if dz:
                comb[g, dz] = value.astype(jnp.bfloat16)
                pending.append(
                    remote(
                        comb.at[g, dz],
                        fin.at[g, dz],
                        rz_send.at[g, dz],
                        rz_recv.at[g, dz],
                        device_at(dz, 0),
                    )
                )
            else:
                fin[g, 0] = value.astype(jnp.bfloat16)

    def finish(g):
        value = fin[g, 0].astype(jnp.float32)
        for dz in range(1, hi):
            arrived(fin.at[g, dz], rz_send.at[g, dz], rz_recv.at[g, dz])
            value += fin[g, dz].astype(jnp.float32)
        out_ref[g] = value.astype(jnp.bfloat16)

    def await_panel(p):
        first = pl.multiple_of((1 - core) * half, LANES)
        if p == 2:
            arrived(wd.at[pl.ds(first, half)], panel_send.at[2, 0], panel_recv.at[2, 0])
            return
        panel_copies[p].wait()
        other_cols = pl.ds(pl.multiple_of(p * full + first, LANES), half)
        for q in range(PARTS):
            part = pl.ds(q * piece, piece)
            arrived(wgu.at[part, other_cols], panel_send.at[p, q], panel_recv.at[p, q])

    def picks_of(slot):
        count = jnp.zeros((1, 1), jnp.float32)
        for g in range(batches):
            marks = tok[g, :, pl.ds(width, LANES)].astype(jnp.float32)
            place = lax.broadcasted_iota(jnp.int32, marks.shape, 1)
            mine = (place >= top) & (place < 2 * top) & (marks == slot.astype(jnp.float32))
            per_lane = jnp.sum(jnp.where(mine, 1.0, 0.0), axis=0, keepdims=True)
            count += jnp.sum(per_lane, axis=1, keepdims=True)
        return count

    send_z(0)
    for p, (src, dst) in enumerate(panels[:2]):
        for q in range(PARTS):
            part = pl.ds(q * piece, piece)
            pending.append(
                remote(
                    src.at[part],
                    dst.at[part],
                    panel_send.at[p, q],
                    panel_recv.at[p, q],
                    sibling,
                )
            )
    panel_copies[2].wait()
    tall = min(ROWS, width)

    @pl.loop(0, width // tall)
    def _(i):
        part = pl.ds(pl.multiple_of(i * tall, tall), tall)
        wd[gate_cols, part] = stage[part, :].T

    turned = wd.at[gate_cols]
    pending.append(remote(turned, turned, panel_send.at[2, 0], panel_recv.at[2, 0], sibling))
    relay_z(0)
    for g in range(1, batches):
        send_z(g)
    await_x(0)
    for g in range(batches):
        if g == 0:
            await_panel(0)
            await_panel(1)
        hidden(g)
        if g == 0:
            await_panel(2)
        result(g)
        if g + 1 < batches:
            relay_z(g + 1)
            await_x(g + 1)
    for g in range(batches):
        collect(g)

    tally[0] = jnp.broadcast_to(picks_of(sibling), tally.shape[1:])
    swap = remote(tally.at[0], tally.at[1], tally_sem.at[0], tally_sem.at[1], sibling)
    pending.append(swap)
    count = picks_of(me)
    for g in range(batches):
        finish(g)
    arrived(tally.at[1], tally_sem.at[0], tally_sem.at[1])
    load_ref[...] = (count + tally[1, :1, :1]).astype(jnp.int32)
    for copy in pending:
        copy.wait_send()


def per_device(
    activations,
    pick_weight,
    expert_ids,
    replica,
    old_home,
    new_expert,
    gate_panel,
    up_panel,
    down_panel,
):
    n = lax.axis_size("expert")
    hi, lo = grid_of(n)
    batches, t, width = activations.shape
    half = gate_panel.shape[2]
    total = hi * lo * t
    dma = pltpu.SemaphoreType.DMA
    vmem = pl.BlockSpec(memory_space=pltpu.VMEM)
    hbm = pl.BlockSpec(memory_space=pl.ANY)
    bf16 = jnp.bfloat16
    out, load = pl.pallas_call(
        functools.partial(layer_kernel, hi, lo),
        out_shape=(
            jax.ShapeDtypeStruct(activations.shape, bf16),
            jax.ShapeDtypeStruct((1, 1), jnp.int32),
        ),
        in_specs=[hbm, vmem, vmem, vmem, vmem, vmem, hbm, hbm, hbm],
        out_specs=(vmem, vmem),
        scratch_shapes=[
            pltpu.VMEM((batches, total, width + LANES), bf16),
            pltpu.VMEM((width, 4 * half), bf16),
            pltpu.VMEM((2 * half, width), bf16),
            pltpu.VMEM((width, half), bf16),
            pltpu.VMEM((batches, total, 2 * half), bf16),
            pltpu.VMEM((batches, total, width), bf16),
            pltpu.VMEM((batches, lo, hi, t, width), bf16),
            pltpu.VMEM((batches, hi, t, width), bf16),
            pltpu.VMEM((batches, hi, t, width), bf16),
            pltpu.VMEM((2, 8, LANES), jnp.float32),
            dma((batches + 3,)),
            dma((3, PARTS)),
            dma((3, PARTS)),
            dma((batches, hi)),
            dma((batches, hi)),
            dma((batches, hi, lo)),
            dma((batches, hi, lo)),
            dma((batches, hi, lo)),
            dma((batches, hi, lo)),
            dma((batches, hi)),
            dma((batches, hi)),
            dma((2,)),
        ],
        compiler_params=pltpu.CompilerParams(
            collective_id=0, has_side_effects=True, vmem_limit_bytes=60 * 1024 * 1024
        ),
        cost_estimate=pl.CostEstimate(
            flops=12 * batches * total * width * half,
            bytes_accessed=12 * width * half,
            transcendentals=2 * batches * total * half,
        ),
        name="expert_layer",
    )(
        activations,
        pick_weight.transpose(0, 2, 1),
        expert_ids.transpose(0, 2, 1),
        replica.transpose(0, 2, 1),
        old_home.reshape(1, -1),
        new_expert.reshape(1, -1),
        gate_panel,
        up_panel,
        down_panel,
    )
    return out, load.reshape(1)


def solution(mesh):
    return jax.shard_map(
        per_device,
        mesh=mesh,
        in_specs=(
            P(None, ("groups", "expert"), None),
            P(None, ("groups", "expert"), None),
            P(None, ("groups", "expert"), None),
            P(None, ("groups", "expert"), None),
            P(),
            P("groups"),
            P("expert", None, None),
            P("expert", None, None),
            P("expert", None, None),
        ),
        out_specs=(P(None, ("groups", "expert"), None), P(("groups", "expert"))),
        check_vma=False,
    )
```
